32 devices in a mesh: grp: 2 (over y), ctx: 8 (over z, x), pair: 2 (over core).
Axes of the slice: x: 2, y: 2, z: 4, core: 2. Of those that a mesh axis runs over, the one named last changes fastest.
Arguments:
- normed_input: bfloat16 [4, 1024, 2688], P(('grp', 'pair'), 'ctx'), parts along dimension 0, may hold values from -6 to 6
- queries: bfloat16 [4, 1024, 2048], P(('grp', 'pair'), 'ctx'), parts along dimension 0, may hold values from -64 to 64
- keys: bfloat16 [4, 1024, 1024], P(('grp', 'pair'), 'ctx'), parts along dimension 0, may hold values from -64 to 64
- value_projection: bfloat16 [2688, 1024], P('ctx'), may hold values from -0.125 to 0.125
- adapter_down: bfloat16 [2688, 16], replicated, may hold values from -0.125 to 0.125
- adapter_up: bfloat16 [16, 1024], replicated, may hold values from -1.5 to 1.5
- output_gradient: bfloat16 [4, 1024, 2048], P(('grp', 'pair'), 'ctx'), parts along dimension 0, may hold values from -6 to 6
- policy_logprob: float32 [4, 1024], P(('grp', 'pair'), 'ctx'), parts along dimension 0, may hold values from -6 to 0
- reference_logprob: float32 [4, 1024], P(('grp', 'pair'), 'ctx'), parts along dimension 0, may hold values from -8 to 0
- token_pair_index: int32 [4, 1024], P(('grp', 'pair'), 'ctx'), parts along dimension 0, may hold values from 0 to 7, never falling along the last dimension, each value on 1 to 1017 neighbouring positions
Outputs:
- input_grad: bfloat16 [4, 1024, 2688], P(('grp', 'pair'), 'ctx'), parts along dimension 0
- query_grad: bfloat16 [4, 1024, 2048], P(('grp', 'pair'), 'ctx'), parts along dimension 0
- key_grad: bfloat16 [4, 1024, 1024], P(('grp', 'pair'), 'ctx'), parts along dimension 0
- down_gradient: float32 [5376, 16], P('grp'), parts along dimension 0
- up_gradient: float32 [32, 1024], P('grp'), parts along dimension 0
The draws below stay inside these ranges and needn't reach their ends.
There are 2 independent parts, one for each index of `grp`. The reference program is written for one: setup_inputs(seed, part) draws one part's arguments, and reference() takes and returns one part's arrays. A program takes and returns all parts, laid end to end along the dimension named above; an argument that names none is the same for every part. Nothing has to cross between parts.
Inputs may be any that keep to these rules, and one draw needn't show every extreme that they name: `token_pair_index`: along each sequence the ids never fall; both sequences hold every id, each segment at most 1017 tokens and one exactly 1017.
All inputs are finite; a program needn't handle non-finite values.
Results may differ from the reference program's by a relative error of at most 0.03.
Values may be sent and summed in bfloat16 or wider, within the bound.
A program may use at most 128 MiB of HBM per device.

```python
import math
import jax
import jax.numpy as jnp
import numpy as np
from jax import lax

MODEL_FEATURES = 2688
HQ = 16
KEY_VALUE_HEADS = 8
HEAD_SIZE = 128
ADAPTER_RANK = 16
WINDOW = 1024
SEGS = 8
TOK_DEV = 128
TOKENS = 1024
SEG_MOST = 1017
N_CTX = 8


def logp_pair(key):
    base = jax.random.fold_in(key, 101)
    first, second = jax.random.split(base)
    policy = -jax.random.uniform(first, (2, TOKENS), jnp.float32, 0.05, 6.0)
    ramp = jnp.arange(TOKENS, dtype=jnp.float32) / TOKENS
    noise = jax.random.normal(second, (2, TOKENS), jnp.float32) * 0.08 * (1.0 + 2.0 * ramp)
    reference = -jnp.abs(policy + noise)
    return (policy, reference)


def draw_policy_logprob(key, part):
    return logp_pair(key)[0]


def draw_reference_logprob(key, part):
    return logp_pair(key)[1]


def query_key_pair(key):
    base = jax.random.fold_in(key, 202)
    first, second = jax.random.split(base)
    query = jnp.clip(jax.random.normal(first, (2, TOKENS, HQ * HEAD_SIZE), jnp.float32), -6.0, 6.0)
    key_vals = jnp.clip(jax.random.normal(second, (2, TOKENS, KEY_VALUE_HEADS * HEAD_SIZE), jnp.float32), -6.0, 6.0)
    return (query, key_vals)


def draw_queries(key, part):
    return query_key_pair(key)[0].astype(jnp.bfloat16)


def draw_keys(key, part):
    return query_key_pair(key)[1].astype(jnp.bfloat16)


def levels(stream_key, shape, cuts, smallest, high):
    factor_of, own = 1.0, jax.random.fold_in(stream_key, 6)
    for axis_at, blocks in cuts:
        steps = jnp.exp(jax.random.uniform(jax.random.fold_in(own, axis_at), (blocks,), jnp.float32, smallest / len(cuts), high / len(cuts)))
        factor_of = factor_of * jnp.repeat(steps, shape[axis_at] // blocks).reshape([-1 if axis == axis_at else 1 for axis in range(len(shape))])
    return factor_of


def split_up(count, total, bound, skew):
    weights = [(1 << 20) // math.isqrt(rank ** skew) + 1 for rank in range(2, count + 1)]
    surplus, holding = total - bound - (count - 1), [1] * (count - 1)
    while surplus > 0:
        candidates = [i for i in range(count - 1) if holding[i] < bound]
        whole, left = sum([weights[i] for i in candidates]), surplus
        for i in candidates:
            addition = min(bound - holding[i], max(1, left * weights[i] // whole), surplus)
            holding[i] = holding[i] + addition
            surplus = surplus - addition
    return np.array([bound] + holding)


def ragged(key, number_of, total, limit, skew):
    if number_of == 2:
        one = jax.random.randint(key, (), max(1, total - limit), min(limit, total - 1) + 1)
        return jnp.stack([one, total - one])
    tallies = jnp.asarray(split_up(number_of, total, limit, skew), jnp.int32)
    couples = (number_of - 1) // 2
    source_of, taker = tallies[1:1 + 2 * couples:2], tallies[2:2 + 2 * couples:2]
    room = jnp.minimum(source_of - 1, limit - taker)
    shifted = jax.random.randint(jax.random.fold_in(key, 1), (couples,), 0, 1 << 20) % (room + 1)
    tallies = tallies.at[1:1 + 2 * couples:2].set(source_of - shifted).at[2:2 + 2 * couples:2].set(taker + shifted)
    return tallies[jax.random.permutation(jax.random.fold_in(key, 2), number_of)]


def centred(rng, shape, scale, most, shards=(), held_as=jnp.bfloat16):
    array = scale * jax.random.normal(rng, shape, jnp.float32)
    if shards:
        array = array * levels(rng, shape, shards, -0.22, 0.18)
    return jnp.clip(array, -most, most).astype(held_as)


def setup_inputs(seed: int = 0, part: int = 0) -> dict:
    seeds = jax.random.split(jax.random.key(seed), 11)
    part_keys = jax.random.split(jax.random.fold_in(seeds[10], part), 11)
    return {
        "normed_input": centred(part_keys[0], (2, TOKENS, MODEL_FEATURES), 1.0, 6.0, ((0, 2), (1, 8))),
        "queries": draw_queries(jax.random.fold_in(jax.random.fold_in(seeds[10], part), 71), part),
        "keys": draw_keys(jax.random.fold_in(jax.random.fold_in(seeds[10], part), 71), part),
        "value_projection": centred(seeds[3], (MODEL_FEATURES, KEY_VALUE_HEADS * HEAD_SIZE), MODEL_FEATURES ** -0.5, 0.125, ((0, 8),)),
        "adapter_down": centred(seeds[4], (MODEL_FEATURES, ADAPTER_RANK), MODEL_FEATURES ** -0.5, 0.125),
        "adapter_up": centred(seeds[5], (ADAPTER_RANK, KEY_VALUE_HEADS * HEAD_SIZE), ADAPTER_RANK ** -0.5, 1.5),
        "output_gradient": centred(part_keys[6], (2, TOKENS, HQ * HEAD_SIZE), 1.0, 6.0, ((0, 2), (1, 8))),
        "policy_logprob": draw_policy_logprob(jax.random.fold_in(jax.random.fold_in(seeds[10], part), 71), part),
        "reference_logprob": draw_reference_logprob(jax.random.fold_in(jax.random.fold_in(seeds[10], part), 71), part),
        "token_pair_index": jax.vmap(lambda own: jnp.searchsorted(jnp.cumsum(ragged(own, SEGS, TOKENS, SEG_MOST, 1)), jnp.arange(TOKENS), side="right"))(jax.random.split(part_keys[9], 2)).reshape((2, TOKENS)).astype(jnp.int32),
    }


DPO_BETA = 0.1
LOSS_SCALE = 256.0
ADAPTER_SCALE = 2.0
ATTN_SCALE = 168.0 ** -0.5
NEG_FILL = -1e30


def sequence_sweep(hidden_rows, query_sequence, key_sequence, output_sequence, segment_labels, token_coefficient, value_projection, adapter_down, adapter_up):
    width_kv = KEY_VALUE_HEADS * HEAD_SIZE
    group_size = HQ // KEY_VALUE_HEADS
    span = WINDOW + TOK_DEV
    rank_projection = jnp.dot(hidden_rows, adapter_down, preferred_element_type=jnp.float32).astype(jnp.bfloat16)
    values = (jnp.dot(hidden_rows, value_projection, preferred_element_type=jnp.float32)
              + ADAPTER_SCALE * jnp.dot(rank_projection, adapter_up, preferred_element_type=jnp.float32)).astype(jnp.bfloat16)
    key_pad = jnp.concatenate([jnp.zeros((WINDOW, width_kv), jnp.bfloat16), key_sequence], 0)
    value_pad = jnp.concatenate([jnp.zeros((WINDOW, width_kv), jnp.bfloat16), values], 0)
    seg_pad = jnp.concatenate([jnp.full((WINDOW,), -1, jnp.int32), segment_labels.astype(jnp.int32)], 0)

    def settle(part):
        far_rows = lax.optimization_barrier(part[:WINDOW].astype(jnp.bfloat16))
        return jnp.concatenate([far_rows.astype(jnp.float32), part[WINDOW:]], 0)

    def block_step(accum, block):
        key_acc, value_acc = accum
        block_start = (block * TOK_DEV).astype(jnp.int32)
        query_blk = lax.dynamic_slice_in_dim(query_sequence, block_start, TOK_DEV, 0).reshape(TOK_DEV, KEY_VALUE_HEADS, group_size, HEAD_SIZE).astype(jnp.float32)
        grad_blk = lax.dynamic_slice_in_dim(output_sequence, block_start, TOK_DEV, 0).reshape(TOK_DEV, KEY_VALUE_HEADS, group_size, HEAD_SIZE).astype(jnp.float32)
        key_blk = lax.dynamic_slice_in_dim(key_pad, block_start, span, 0).reshape(span, KEY_VALUE_HEADS, HEAD_SIZE).astype(jnp.float32)
        value_blk = lax.dynamic_slice_in_dim(value_pad, block_start, span, 0).reshape(span, KEY_VALUE_HEADS, HEAD_SIZE).astype(jnp.float32)
        seg_query = lax.dynamic_slice_in_dim(segment_labels.astype(jnp.int32), block_start, TOK_DEV, 0)
        seg_key = lax.dynamic_slice_in_dim(seg_pad, block_start, span, 0)
        coef_blk = lax.dynamic_slice_in_dim(token_coefficient, block_start, TOK_DEV, 0)[None, None, :, None]
        tpos = block_start + jnp.arange(TOK_DEV, dtype=jnp.int32)
        upos = block_start - WINDOW + jnp.arange(span, dtype=jnp.int32)
        allowed = (upos[None, :] <= tpos[:, None]) & (upos[None, :] > tpos[:, None] - WINDOW) & (seg_key[None, :] == seg_query[:, None])
        scores = ATTN_SCALE * jnp.einsum('tjgd,ljd->jgtl', query_blk, key_blk)
        masked = jnp.where(allowed[None, None], scores, NEG_FILL)
        row_max = jnp.max(masked, -1, keepdims=True)
        weights_exp = jnp.where(allowed[None, None], jnp.exp(masked - row_max), 0.0)
        attn_probs = weights_exp / jnp.sum(weights_exp, -1, keepdims=True)
        prob_grad = coef_blk * jnp.einsum('tjgd,ljd->jgtl', grad_blk, value_blk)
        row_delta = jnp.sum(attn_probs * prob_grad, -1, keepdims=True)
        score_grad = (ATTN_SCALE * attn_probs * (prob_grad - row_delta)).astype(jnp.bfloat16)
        query_grad = jnp.einsum('jgtl,ljd->tjgd', score_grad.astype(jnp.float32), key_blk).reshape(TOK_DEV, HQ * HEAD_SIZE).astype(jnp.bfloat16)
        key_part = jnp.einsum('jgtl,tjgd->ljd', score_grad.astype(jnp.float32), query_blk).reshape(span, width_kv)
        weighted = (attn_probs * coef_blk).astype(jnp.bfloat16)
        value_part = jnp.einsum('jgtl,tjgd->ljd', weighted.astype(jnp.float32), grad_blk).reshape(span, width_kv)
        key_acc = lax.dynamic_update_slice_in_dim(key_acc, lax.dynamic_slice_in_dim(key_acc, block_start, span, 0) + settle(key_part), block_start, 0)
        value_acc = lax.dynamic_update_slice_in_dim(value_acc, lax.dynamic_slice_in_dim(value_acc, block_start, span, 0) + settle(value_part), block_start, 0)
        return (key_acc, value_acc), query_grad

    accum_init = (jnp.zeros((TOKENS + WINDOW, width_kv), jnp.float32), jnp.zeros((TOKENS + WINDOW, width_kv), jnp.float32))
    (key_acc, value_acc), query_blocks = lax.scan(block_step, accum_init, jnp.arange(N_CTX, dtype=jnp.int32))
    query_grad = query_blocks.reshape(TOKENS, HQ * HEAD_SIZE)
    key_grad = key_acc[WINDOW:].astype(jnp.bfloat16)
    value_gradient = value_acc[WINDOW:].astype(jnp.bfloat16)
    rank_middle = jnp.dot(value_gradient, adapter_up.T, preferred_element_type=jnp.float32).astype(jnp.bfloat16)
    input_grad = (jnp.dot(value_gradient, value_projection.T, preferred_element_type=jnp.float32)
                  + ADAPTER_SCALE * jnp.dot(rank_middle, adapter_down.T, preferred_element_type=jnp.float32)).astype(jnp.bfloat16)
    up_factor = jnp.dot(rank_projection.T, value_gradient, preferred_element_type=jnp.float32)
    down_factor = jnp.dot(hidden_rows.T, rank_middle, preferred_element_type=jnp.float32)
    return input_grad, query_grad, key_grad, down_factor, up_factor


def reference(normed_input, queries, keys, value_projection, adapter_down, adapter_up, output_gradient, policy_logprob, reference_logprob, token_pair_index):
    diff_sums = jnp.stack([
        jax.ops.segment_sum(policy_logprob[pair_position] - reference_logprob[pair_position], token_pair_index[pair_position], num_segments=SEGS)
        for pair_position in range(2)], 0)
    margin = DPO_BETA * (diff_sums[0] - diff_sums[1])
    sig_term = jax.nn.sigmoid(-margin)
    coef = jnp.stack([-DPO_BETA * LOSS_SCALE * sig_term, DPO_BETA * LOSS_SCALE * sig_term], 0)
    input_list = []
    query_list = []
    key_list = []
    down_gradient = jnp.zeros((MODEL_FEATURES, ADAPTER_RANK), jnp.float32)
    up_gradient = jnp.zeros((ADAPTER_RANK, KEY_VALUE_HEADS * HEAD_SIZE), jnp.float32)
    for pair_position in range(2):
        token_coefficient = coef[pair_position][token_pair_index[pair_position]]
        input_grad, query_grad, key_grad, down_factor, up_factor = sequence_sweep(
            normed_input[pair_position], queries[pair_position], keys[pair_position], output_gradient[pair_position],
            token_pair_index[pair_position], token_coefficient, value_projection, adapter_down, adapter_up)
        input_list.append(input_grad)
        query_list.append(query_grad)
        key_list.append(key_grad)
        down_gradient = down_gradient + down_factor
        up_gradient = up_gradient + up_factor
    down_gradient = ADAPTER_SCALE * down_gradient
    up_gradient = ADAPTER_SCALE * up_gradient
    return (jnp.stack(input_list, 0), jnp.stack(query_list, 0), jnp.stack(key_list, 0), down_gradient, up_gradient)
```

```python
import functools

import jax
import jax.numpy as jnp
from jax import lax
from jax.experimental import pallas as pl
from jax.experimental.pallas import tpu as pltpu
from jax.sharding import PartitionSpec as P

HEAD = 128
WINDOW = 1024
SEGS = 8
BETA = 0.1
LOSS = 256.0
ADAPT = 2.0
SCALE = 168.0**-0.5
NEG = -1e30
MESH = pl.DeviceIdType.MESH
F32 = jnp.float32
BF16 = jnp.bfloat16


def mm(a, b, ca, cb):
    return lax.dot_general(a, b, (((ca,), (cb,)), ((), ())), preferred_element_type=F32)


def kernel(
    n, L, D, NC, LOG,
    x_ref, q_ref, k_ref, w_ref, dn_ref, up_ref, g_ref, lab_ref, gap_ref,
    xg_ref, qg_ref, kg_ref, dd_ref, du_ref,
    wb, kb, vb, lb, sb, bias, lowr, pb, own, xr, zr, zs,
    hd, hu, rd, ru, crow,
    wring_s, wring_r, wpair_s, wpair_r,
    kz_s, kx_s, k_r, vz_s, vx_s, v_r, l_s, l_r, s_s, s_r,
    px_s, px_r, pz_s, pz_r, rd_s, rd_r, ru_s, ru_r,
):
    c = lax.axis_index("ctx")
    p = lax.axis_index("pair")
    even = lax.rem(c, 2) == 0
    odd = lax.rem(c, 2) == 1
    T = k_ref.shape[0]
    CW = k_ref.shape[1] // NC
    HALF = k_ref.shape[1] // 2

    def remote(src, dst, ss, rs, ctx, pair):
        return pltpu.make_async_remote_copy(
            src_ref=src, dst_ref=dst, send_sem=ss, recv_sem=rs,
            device_id={"ctx": ctx, "pair": pair}, device_id_type=MESH)

    barrier = pltpu.get_barrier_semaphore()
    me = c * 2 + p

    def greet(i, _):
        other = lax.rem(me + i, 2 * n)
        pl.semaphore_signal(barrier, inc=1, device_id={"ctx": other // 2, "pair": lax.rem(other, 2)},
                            device_id_type=MESH)
        return 0
    lax.fori_loop(1, 2 * n, greet, 0)
    pl.semaphore_wait(barrier, 2 * n - 1)

    pos = jnp.where(even, c // 2, n - 1 - c // 2)

    def at(position):
        r = lax.rem(position + 2 * n, n)
        return jnp.where(r < n // 2, 2 * r, 2 * (n - 1 - r) + 1)
    right, left = at(pos + 1), at(pos - 1)
    NR = n // 2
    NL = n - 1 - NR

    def hop(direction, slot, src, to):
        return remote(src, wb.at[slot, p], wring_s.at[direction, slot], wring_r.at[slot], to, p)

    def to_partner(slot):
        return remote(wb.at[slot, p], wb.at[slot, p], wpair_s.at[slot], wpair_r.at[slot], c, 1 - p)

    hop(0, c, w_ref.at[p], right).start()
    hop(1, c, w_ref.at[p], left).start()

    onehot = (lab_ref[...] == lax.broadcasted_iota(jnp.int32, (SEGS, T), 0).astype(F32)).astype(F32)
    part = jnp.sum(onehot * gap_ref[...], axis=1, keepdims=True)
    sb[p, c] = jnp.broadcast_to(part, (SEGS, 128))
    lb[0] = lab_ref[...]

    def sums(i):
        other = lax.rem(me + i, 2 * n)
        return remote(sb.at[p, c], sb.at[p, c], s_s.at[i], s_r.at[p, c], other // 2, lax.rem(other, 2))

    def send_sums(i, _):
        sums(i).start()
        return 0
    lax.fori_loop(1, 2 * n, send_sums, 0)

    def label(d):
        return remote(lb.at[0], lb.at[d], l_s.at[d], l_r.at[d], c + d, p)
    for d in range(1, D + 1):
        @pl.when(c + d < n)
        def _():
            label(d).start()

        @pl.when(c - d < 0)
        def _():
            kb[d] = jnp.zeros_like(kb[d])
            vb[d] = jnp.zeros_like(vb[d])
            lb[d] = jnp.full_like(lb[d], -1.0)

    def chain(buf, zs_, xs_, rs_, src, cols, ch):
        def cut(ref):
            return ref if cols is None else ref.at[:, cols]

        def z(k):
            return remote(cut(src if k == 0 else buf.at[2 * k]), cut(buf.at[2 * k + 2]), zs_.at[ch, k],
                          rs_.at[ch, 2 * k + 2], c + 2, p)

        def xe(k):
            return remote(cut(src if k == 0 else buf.at[2 * k]), cut(buf.at[2 * k + 1]), xs_.at[ch, k],
                          rs_.at[ch, 2 * k + 1], c + 1, p)

        def xo(k):
            return remote(cut(buf.at[2 * k]), cut(buf.at[2 * k - 1]), xs_.at[ch, k], rs_.at[ch, 2 * k - 1], c - 1, p)

        def each(k, do):
            if k < L:
                @pl.when((c + 2 < n) & (c - 2 * k >= 0))
                def _():
                    do(z(k))
            if 2 * k + 1 <= D:
                @pl.when(even & (c - 2 * k >= 0))
                def _():
                    do(xe(k))
            if k >= 1:
                @pl.when(odd & (c - 2 * k >= 0))
                def _():
                    do(xo(k))

        def arrived(d):
            @pl.when(c - d >= 0)
            def _():
                remote(cut(buf.at[d]), cut(buf.at[d]), zs_.at[ch, 0], rs_.at[ch, d], c - d, p).wait_recv()

        def step(k):
            if k >= 1:
                arrived(2 * k)
            each(k, lambda copy: copy.start())

        def rest():
            for d in range(1, D + 1, 2):
                arrived(d)

        def sent():
            for k in range(L + 1):
                each(k, lambda copy: copy.wait_send())
        return step, rest, sent

    k_step, k_rest, k_sent = chain(kb, kz_s, kx_s, k_r, k_ref, None, 0)
    k_step(0)
    kb[0] = k_ref[...]
    wb[c] = w_ref[...]

    def low_part(j, acc):
        return acc + mm(x_ref[j], dn_ref[j], 1, 0)
    lowr[...] = lax.fori_loop(0, n, low_part, jnp.zeros(lowr.shape, F32)).astype(BF16)

    def ring_step(s):
        slot = at(pos - s)
        hop(0, slot, wb.at[slot, p], right).wait_recv()

        @pl.when(s < NR)
        def _():
            hop(0, slot, wb.at[slot, p], right).start()
        to_partner(slot).start()

        @pl.when(s <= NL)
        def _():
            slot2 = at(pos + s)
            hop(1, slot2, wb.at[slot2, p], left).wait_recv()

            @pl.when(s < NL)
            def _():
                hop(1, slot2, wb.at[slot2, p], left).start()
            to_partner(slot2).start()

    if n <= 16:
        for s in range(1, NR + 1):
            ring_step(jnp.int32(s))
            if s <= L:
                k_step(s)
        for s in range(NR + 1, L + 1):
            k_step(s)
    else:
        def ring_body(s, _):
            ring_step(s)
            return 0
        lax.fori_loop(1, NR + 1, ring_body, 0)
        for s in range(1, L + 1):
            k_step(s)

    def partner_in(i, _):
        to_partner(lax.rem(c + i, n)).wait_recv()
        return 0
    lax.fori_loop(1, n, partner_in, 0)

    v_chains = []
    for ch in range(NC):
        lo = ch * CW
        cols = slice(lo, lo + CW)
        half, inner = lo // HALF, lo % HALF

        def value_part(j, acc):
            return acc + mm(x_ref[j], wb[j, half, :, inner:inner + CW], 1, 0)
        acc = lax.fori_loop(0, n, value_part, ADAPT * mm(lowr[...], up_ref[:, cols], 1, 0))
        vb[0, :, cols] = acc.astype(BF16)
        steps = chain(vb, vz_s, vx_s, v_r, vb.at[0], pl.ds(lo, CW), ch)
        v_chains.append(steps)
        steps[0](0)

    def sums_in(i, _):
        other = lax.rem(me + i, 2 * n)
        remote(sb.at[0, 0], sb.at[lax.rem(other, 2), other // 2], s_s.at[i], s_r.at[lax.rem(other, 2), other // 2],
               other // 2, lax.rem(other, 2)).wait_recv()
        return 0
    lax.fori_loop(1, 2 * n, sums_in, 0)
    margin = BETA * (jnp.sum(sb[0], axis=0) - jnp.sum(sb[1], axis=0))
    sign = 2.0 * p.astype(F32) - 1.0
    coef = sign * (BETA * LOSS) * jax.nn.sigmoid(-margin)
    token_coef = jnp.sum(onehot * coef, axis=0, keepdims=True)
    crow[...] = jnp.broadcast_to(jnp.concatenate([token_coef, token_coef], axis=1), crow.shape)

    lq = lab_ref[0:1, :]
    for d in range(D + 1):
        if d:
            @pl.when(c - d >= 0)
            def _():
                remote(lb.at[d], lb.at[d], l_s.at[d], l_r.at[d], c - d, p).wait_recv()
        lk = jnp.transpose(jnp.broadcast_to(lb[d][0:1, :], (T, T)))
        apart = (d * T + lax.broadcasted_iota(jnp.int32, (T, T), 1) - lax.broadcasted_iota(jnp.int32, (T, T), 0))
        ok = (lk == lq) & (apart >= 0) & (apart < WINDOW)
        b = jnp.where(ok, 0.0, NEG)
        bias[d * T:(d + 1) * T, :] = jnp.concatenate([b, b], axis=1)

    for k in range(1, L + 1):
        for ch in range(NC):
            v_chains[ch][0](k)
    k_rest()

    S = (D + 1) * T
    HC = CW // HEAD

    def px(ch, k, d, to):
        cs = pl.ds(ch * CW, CW)
        return remote(pb.at[d, :, :, cs], xr.at[k, :, :, cs], px_s.at[ch, k], px_r.at[ch, k], to, p)

    def parts_each(ch, do):
        for k in range(L + 1):
            if k >= 1:
                @pl.when(even & (c - 2 * k + 1 >= 0))
                def _():
                    do(px(ch, k, 2 * k - 1, c + 1))
            if 2 * k + 1 <= D:
                @pl.when(odd & (c - 2 * k - 1 >= 0))
                def _():
                    do(px(ch, k, 2 * k + 1, c - 1))

    def pz(ch, k):
        cs = pl.ds(ch * CW, CW)
        return remote(zs.at[k, :, :, cs], zr.at[k, :, :, cs], pz_s.at[ch, k], pz_r.at[ch, k], c - 2, p)

    def x_in(ch, k):
        px(ch, k, k, jnp.where(even, c + 1, c - 1)).wait_recv()

    def sum_chain(ch):
        cs = slice(ch * CW, (ch + 1) * CW)
        for k in range(L, -1, -1):
            @pl.when(c - 2 * k >= 0)
            def _():
                @pl.when(odd if 2 * k + 1 > D else (even if k == 0 else c >= 0))
                def _():
                    x_in(ch, k)
                if k + 1 <= L:
                    @pl.when(c + 2 < n)
                    def _():
                        pz(ch, k + 1).wait_recv()
                total = own[:, :, cs] if k == 0 else pb[2 * k, :, :, cs].astype(F32)
                use_x = odd if 2 * k + 1 > D else (even if k == 0 else c >= 0)
                total = total + jnp.where(use_x, xr[k, :, :, cs].astype(F32), 0.0)
                if k + 1 <= L:
                    total = total + jnp.where(c + 2 < n, zr[k + 1, :, :, cs].astype(F32), 0.0)
                if k == 0:
                    own[:, :, cs] = total
                else:
                    zs[k, :, :, cs] = total.astype(BF16)
                    pz(ch, k).start()

    for ch in range(NC):
        v_chains[ch][1]()

        def head(i, _):
            j = ch * HC + i
            hc = pl.ds(pl.multiple_of(j * HEAD, HEAD), HEAD)
            qa = pl.ds(pl.multiple_of(j * 2 * HEAD, HEAD), HEAD)
            qb = pl.ds(pl.multiple_of(j * 2 * HEAD + HEAD, HEAD), HEAD)
            qh = jnp.concatenate([q_ref[:, qa], q_ref[:, qb]], axis=0)
            gh = jnp.concatenate([g_ref[:, qa], g_ref[:, qb]], axis=0)
            kh = kb[:, :, hc].reshape(S, HEAD)
            vh = vb[:, :, hc].reshape(S, HEAD)
            cr = crow[0:1, :]
            s = mm(kh, qh, 1, 1) * SCALE + bias[...]
            e = jnp.exp(s - jnp.max(s, axis=0, keepdims=True))
            probs = e * (1.0 / jnp.sum(e, axis=0, keepdims=True))
            dp = mm(vh, gh, 1, 1) * cr
            delta = jnp.sum(probs * dp, axis=0, keepdims=True)
            ds = (SCALE * probs * (dp - delta)).astype(BF16)
            wt = (probs * cr).astype(BF16)
            dq = mm(ds, kh, 0, 0).astype(BF16)
            qg_ref[:, qa] = dq[:T]
            qg_ref[:, qb] = dq[T:]
            dk = mm(ds, qh, 1, 0)
            dv = mm(wt, gh, 1, 0)
            own[0, :, hc] = dk[:T]
            own[1, :, hc] = dv[:T]
            pb[1:, 0, :, hc] = dk[T:].astype(BF16).reshape(D, T, HEAD)
            pb[1:, 1, :, hc] = dv[T:].astype(BF16).reshape(D, T, HEAD)
            return 0
        lax.fori_loop(0, HC, head, 0)
        parts_each(ch, lambda copy: copy.start())
        if ch >= 1:
            sum_chain(ch - 1)
    sum_chain(NC - 1)

    kg_ref[...] = own[0].astype(BF16)
    vg = own[1].astype(BF16)
    mid = mm(vg, up_ref[...], 1, 1).astype(BF16)
    uf = ADAPT * mm(lowr[...], vg, 0, 0)
    for h in range(2):
        hu[h] = uf[:, h * HALF:(h + 1) * HALF]
    nh = n // 2

    def down_part(j, _):
        hd[j // nh, lax.rem(j, nh)] = ADAPT * mm(mid, x_ref[j], 0, 0)
        return 0
    lax.fori_loop(0, n, down_part, 0)

    def both(i, src, to, pair):
        return (remote(hd.at[src], rd.at[i], rd_s.at[i], rd_r.at[i], to, pair),
                remote(hu.at[src], ru.at[i], ru_s.at[i], ru_r.at[i], to, pair))

    def grad_part(j, _):
        g = mm(vg[:, :HALF], wb[j, 0], 1, 1) + mm(vg[:, HALF:], wb[j, 1], 1, 1)
        xg_ref[j] = (g + ADAPT * mm(mid, dn_ref[j], 1, 1)).astype(BF16)
        return 0

    rounds = LOG + 2
    for i in range(rounds):
        if i == 0:
            copies = both(i, 1 - p, c, 1 - p)
        elif i <= LOG:
            bit = 1 << (i - 1)
            to = jnp.where(lax.rem(c // bit, 2) == 0, c + bit, c - bit)
            copies = both(i, p, to, p)
        else:
            copies = both(i, p, c, 1 - p)
        for copy in copies:
            copy.start()
        lax.fori_loop(n * i // rounds, n * (i + 1) // rounds, grad_part, 0)
        for copy in copies:
            copy.wait()
        if i <= LOG:
            hd[p] = hd[p] + rd[i]
            hu[p] = hu[p] + ru[i]
    dd_ref[p] = hd[p]
    du_ref[p] = hu[p]
    dd_ref[1 - p] = rd[rounds - 1]
    du_ref[1 - p] = ru[rounds - 1]

    hop(0, c, w_ref.at[p], right).wait_send()
    hop(1, c, w_ref.at[p], left).wait_send()

    def ring_sent(s, _):
        slot = at(pos - s)

        @pl.when(s < NR)
        def _():
            hop(0, slot, wb.at[slot, p], right).wait_send()
        to_partner(slot).wait_send()

        @pl.when(s <= NL)
        def _():
            slot2 = at(pos + s)

            @pl.when(s < NL)
            def _():
                hop(1, slot2, wb.at[slot2, p], left).wait_send()
            to_partner(slot2).wait_send()
        return 0
    lax.fori_loop(1, NR + 1, ring_sent, 0)

    def sums_sent(i, _):
        sums(i).wait_send()
        return 0
    lax.fori_loop(1, 2 * n, sums_sent, 0)
    for d in range(1, D + 1):
        @pl.when(c + d < n)
        def _():
            label(d).wait_send()
    k_sent()
    for ch in range(NC):
        v_chains[ch][2]()
        parts_each(ch, lambda copy: copy.wait_send())
        for k in range(1, L + 1):
            @pl.when(c - 2 * k >= 0)
            def _():
                pz(ch, k).wait_send()


def shards(x, q, k, w, dn, up, g, plp, rlp, idx):
    n = lax.axis_size("ctx")
    T, width = k.shape[1], k.shape[2]
    rows = w.shape[0]
    R = -(-rows // 16) * 16
    model = x.shape[2]
    halo = WINDOW // T
    D = min(halo, n - 1)
    L = min(halo // 2, n // 2 - 1)
    NC = 4
    LOG = n.bit_length() - 1
    HALF = width // 2
    pad = R - rows
    xs = jnp.pad(x[0].reshape(T, n, rows).transpose(1, 0, 2), ((0, 0), (0, 0), (0, pad)))
    ws = jnp.pad(w.reshape(rows, 2, HALF).transpose(1, 0, 2), ((0, 0), (0, pad), (0, 0)))
    dns = jnp.pad(dn.reshape(n, rows, dn.shape[1]), ((0, 0), (0, pad), (0, 0)))
    lab = jnp.broadcast_to(idx.astype(F32), (SEGS, T))
    gap = jnp.broadcast_to(plp - rlp, (SEGS, T))
    rank = dn.shape[1]
    vm = pl.BlockSpec(memory_space=pltpu.VMEM)
    dma = pltpu.SemaphoreType.DMA
    xg, qg, kg, dd, du = pl.pallas_call(
        functools.partial(kernel, n, L, D, NC, LOG),
        out_shape=(
            jax.ShapeDtypeStruct((n, T, R), BF16),
            jax.ShapeDtypeStruct(q.shape[1:], BF16),
            jax.ShapeDtypeStruct(k.shape[1:], BF16),
            jax.ShapeDtypeStruct((2, n // 2, rank, R), F32),
            jax.ShapeDtypeStruct((2, rank, HALF), F32),
        ),
        in_specs=[vm] * 9,
        out_specs=[vm] * 5,
        scratch_shapes=[
            pltpu.VMEM((n, 2, R, HALF), BF16),
            pltpu.VMEM((D + 1, T, width), BF16),
            pltpu.VMEM((D + 1, T, width), BF16),
            pltpu.VMEM((D + 1, SEGS, T), F32),
            pltpu.VMEM((2, n, SEGS, 128), F32),
            pltpu.VMEM(((D + 1) * T, 2 * T), F32),
            pltpu.VMEM((T, rank), BF16),
            pltpu.VMEM((D + 1, 2, T, width), BF16),
            pltpu.VMEM((2, T, width), F32),
            pltpu.VMEM((L + 1, 2, T, width), BF16),
            pltpu.VMEM((L + 1, 2, T, width), BF16),
            pltpu.VMEM((L + 1, 2, T, width), BF16),
            pltpu.VMEM((2, n // 2, rank, R), F32),
            pltpu.VMEM((2, rank, HALF), F32),
            pltpu.VMEM((LOG + 2, n // 2, rank, R), F32),
            pltpu.VMEM((LOG + 2, rank, HALF), F32),
            pltpu.VMEM((8, 2 * T), F32),
            dma((2, n)), dma((n,)), dma((n,)), dma((n,)),
            dma((1, L + 1)), dma((1, L + 1)), dma((1, D + 1)),
            dma((NC, L + 1)), dma((NC, L + 1)), dma((NC, D + 1)),
            dma((D + 1,)), dma((D + 1,)), dma((2 * n,)), dma((2, n)),
            dma((NC, L + 1)), dma((NC, L + 1)), dma((NC, L + 1)), dma((NC, L + 1)),
            dma((LOG + 2,)), dma((LOG + 2,)), dma((LOG + 2,)), dma((LOG + 2,)),
        ],
        compiler_params=pltpu.CompilerParams(
            collective_id=0, has_side_effects=True, vmem_limit_bytes=60 * 1024 * 1024),
    )(xs, q[0], k[0], ws, dns, up, g[0], lab, gap)
    input_grad = xg[:, :, :rows].transpose(1, 0, 2).reshape(T, model)
    down = dd.reshape(n, rank, R)[:, :, :rows].transpose(0, 2, 1).reshape(model, rank)
    upg = du.transpose(1, 0, 2).reshape(rank, width)
    return input_grad[None], qg[None], kg[None], down, upg


def solution(mesh):
    tok = P(("grp", "pair"), "ctx", None)
    row = P(("grp", "pair"), "ctx")
    return jax.shard_map(
        shards,
        mesh=mesh,
        in_specs=(tok, tok, tok, P("ctx", None), P(), P(), tok, row, row, row),
        out_specs=(tok, tok, tok, P("grp", None), P("grp", None)),
        check_vma=False,
    )
```

```python
import functools

import jax
import jax.numpy as jnp
from jax import lax
from jax.experimental import pallas as pl
from jax.experimental.pallas import tpu as pltpu
from jax.sharding import PartitionSpec as P

HEAD = 128
WINDOW = 1024
SEGS = 8
BETA = 0.1
LOSS = 256.0
ADAPT = 2.0
SCALE = 168.0**-0.5
NEG = -1e30
MESH = pl.DeviceIdType.MESH
F32 = jnp.float32
BF16 = jnp.bfloat16


def mm(a, b, ca, cb):
    return lax.dot_general(a, b, (((ca,), (cb,)), ((), ())), preferred_element_type=F32)


def kernel(
    n, L, D, NC, LOG,
    x_ref, q_ref, k_ref, w_ref, dn_ref, up_ref, g_ref, lab_ref, gap_ref,
    xg_ref, qg_ref, kg_ref, dd_ref, du_ref,
    wb, kb, vb, lb, sb, bias, lowr, pb, own, xr, zr, zs,
    hd, hu, hdb, hub, rd, ru, rfd, rfu, crow,
    wring_s, wring_r, wpair_s, wpair_r,
    kz_s, kx_s, k_r, vz_s, vx_s, v_r, l_s, l_r, s_s, s_r,
    px_s, px_r, pz_s, pz_r, rd_s, rd_r, ru_s, ru_r,
):
    c = lax.axis_index("ctx")
    p = lax.axis_index("pair")
    even = lax.rem(c, 2) == 0
    odd = lax.rem(c, 2) == 1
    T = k_ref.shape[0]
    CW = k_ref.shape[1] // NC
    HALF = k_ref.shape[1] // 2
    M = x_ref.shape[1]
    R = M // n

    def block(slot):
        return wb.at[p, pl.ds(pl.multiple_of(slot * R, 16), R), :]

    def remote(src, dst, ss, rs, ctx, pair):
        return pltpu.make_async_remote_copy(
            src_ref=src, dst_ref=dst, send_sem=ss, recv_sem=rs,
            device_id={"ctx": ctx, "pair": pair}, device_id_type=MESH)

    barrier = pltpu.get_barrier_semaphore()
    me = c * 2 + p

    def greet(i, _):
        other = lax.rem(me + i, 2 * n)
        pl.semaphore_signal(barrier, inc=1, device_id={"ctx": other // 2, "pair": lax.rem(other, 2)},
                            device_id_type=MESH)
        return 0
    lax.fori_loop(1, 2 * n, greet, 0)
    pl.semaphore_wait(barrier, 2 * n - 1)

    pos = jnp.where(even, c // 2, n - 1 - c // 2)

    def at(position):
        r = lax.rem(position + 2 * n, n)
        return jnp.where(r < n // 2, 2 * r, 2 * (n - 1 - r) + 1)
    right, left = at(pos + 1), at(pos - 1)
    NR = n // 2
    NL = n - 1 - NR

    def hop(direction, slot, src, to):
        return remote(src, block(slot), wring_s.at[direction, slot], wring_r.at[slot], to, p)

    def to_partner(slot):
        return remote(block(slot), block(slot), wpair_s.at[slot], wpair_r.at[slot], c, 1 - p)

    hop(0, c, w_ref.at[p], right).start()
    hop(1, c, w_ref.at[p], left).start()

    onehot = (lab_ref[...] == lax.broadcasted_iota(jnp.int32, (SEGS, T), 0).astype(F32)).astype(F32)
    part = jnp.sum(onehot * gap_ref[...], axis=1, keepdims=True)
    sb[p, c] = jnp.broadcast_to(part, (SEGS, 128))
    lb[0] = lab_ref[...]

    def sums(i):
        other = lax.rem(me + i, 2 * n)
        return remote(sb.at[p, c], sb.at[p, c], s_s.at[i], s_r.at[p, c], other // 2, lax.rem(other, 2))

    def send_sums(i, _):
        sums(i).start()
        return 0
    lax.fori_loop(1, 2 * n, send_sums, 0)

    def label(d):
        return remote(lb.at[0], lb.at[d], l_s.at[d], l_r.at[d], c + d, p)
    for d in range(1, D + 1):
        @pl.when(c + d < n)
        def _():
            label(d).start()

        @pl.when(c - d < 0)
        def _():
            kb[d] = jnp.zeros_like(kb[d])
            vb[d] = jnp.zeros_like(vb[d])
            lb[d] = jnp.full_like(lb[d], -1.0)

    def chain(buf, zs_, xs_, rs_, src, cols, ch):
        def cut(ref):
            return ref if cols is None else ref.at[:, cols]

        def z(k):
            return remote(cut(src if k == 0 else buf.at[2 * k]), cut(buf.at[2 * k + 2]), zs_.at[ch, k],
                          rs_.at[ch, 2 * k + 2], c + 2, p)

        def xe(k):
            return remote(cut(src if k == 0 else buf.at[2 * k]), cut(buf.at[2 * k + 1]), xs_.at[ch, k],
                          rs_.at[ch, 2 * k + 1], c + 1, p)

        def xo(k):
            return remote(cut(buf.at[2 * k]), cut(buf.at[2 * k - 1]), xs_.at[ch, k], rs_.at[ch, 2 * k - 1], c - 1, p)

        def each(k, do):
            if k < L:
                @pl.when((c + 2 < n) & (c - 2 * k >= 0))
                def _():
                    do(z(k))
            if 2 * k + 1 <= D:
                @pl.when(even & (c - 2 * k >= 0))
                def _():
                    do(xe(k))
            if k >= 1:
                @pl.when(odd & (c - 2 * k >= 0))
                def _():
                    do(xo(k))

        def arrived(d):
            @pl.when(c - d >= 0)
            def _():
                remote(cut(buf.at[d]), cut(buf.at[d]), zs_.at[ch, 0], rs_.at[ch, d], c - d, p).wait_recv()

        def step(k):
            if k >= 1:
                arrived(2 * k)
            each(k, lambda copy: copy.start())

        def rest():
            for d in range(1, D + 1, 2):
                arrived(d)

        def sent():
            for k in range(L + 1):
                each(k, lambda copy: copy.wait_send())
        return step, rest, sent

    k_step, k_rest, k_sent = chain(kb, kz_s, kx_s, k_r, k_ref, None, 0)
    k_step(0)
    kb[0] = k_ref[...]
    for h in range(2):
        wb[h, pl.ds(pl.multiple_of(c * R, 16), R), :] = w_ref[h]

    lowr[...] = mm(x_ref[...], dn_ref[...], 1, 0).astype(BF16)

    def ring_step(s):
        slot = at(pos - s)
        hop(0, slot, block(slot), right).wait_recv()

        @pl.when(s < NR)
        def _():
            hop(0, slot, block(slot), right).start()
        to_partner(slot).start()

        @pl.when(s <= NL)
        def _():
            slot2 = at(pos + s)
            hop(1, slot2, block(slot2), left).wait_recv()

            @pl.when(s < NL)
            def _():
                hop(1, slot2, block(slot2), left).start()
            to_partner(slot2).start()

    if n <= 16:
        for s in range(1, NR + 1):
            ring_step(jnp.int32(s))
            if s <= L:
                k_step(s)
        for s in range(NR + 1, L + 1):
            k_step(s)
    else:
        def ring_body(s, _):
            ring_step(s)
            return 0
        lax.fori_loop(1, NR + 1, ring_body, 0)
        for s in range(1, L + 1):
            k_step(s)

    def partner_in(i, _):
        to_partner(lax.rem(c + i, n)).wait_recv()
        return 0
    lax.fori_loop(1, n, partner_in, 0)

    v_chains = []
    for ch in range(NC):
        lo = ch * CW
        cols = slice(lo, lo + CW)
        half, inner = lo // HALF, lo % HALF

        acc = mm(x_ref[...], wb[half, :, inner:inner + CW], 1, 0) + ADAPT * mm(lowr[...], up_ref[:, cols], 1, 0)
        vb[0, :, cols] = acc.astype(BF16)
        steps = chain(vb, vz_s, vx_s, v_r, vb.at[0], pl.ds(lo, CW), ch)
        v_chains.append(steps)
        steps[0](0)

    def sums_in(i, _):
        other = lax.rem(me + i, 2 * n)
        remote(sb.at[0, 0], sb.at[lax.rem(other, 2), other // 2], s_s.at[i], s_r.at[lax.rem(other, 2), other // 2],
               other // 2, lax.rem(other, 2)).wait_recv()
        return 0
    lax.fori_loop(1, 2 * n, sums_in, 0)
    margin = BETA * (jnp.sum(sb[0], axis=0) - jnp.sum(sb[1], axis=0))
    sign = 2.0 * p.astype(F32) - 1.0
    coef = sign * (BETA * LOSS) * jax.nn.sigmoid(-margin)
    token_coef = jnp.sum(onehot * coef, axis=0, keepdims=True)
    crow[...] = jnp.broadcast_to(jnp.concatenate([token_coef, token_coef], axis=1), crow.shape)

    lq = lab_ref[0:1, :]
    for d in range(D + 1):
        if d:
            @pl.when(c - d >= 0)
            def _():
                remote(lb.at[d], lb.at[d], l_s.at[d], l_r.at[d], c - d, p).wait_recv()
        lk = jnp.transpose(jnp.broadcast_to(lb[d][0:1, :], (T, T)))
        apart = (d * T + lax.broadcasted_iota(jnp.int32, (T, T), 1) - lax.broadcasted_iota(jnp.int32, (T, T), 0))
        ok = (lk == lq) & (apart >= 0) & (apart < WINDOW)
        b = jnp.where(ok, 0.0, NEG)
        bias[d * T:(d + 1) * T, :] = jnp.concatenate([b, b], axis=1)

    def values_up(ch):
        for k in range(1, L + 1):
            v_chains[ch][0](k)

    values_up(0)
    k_rest()

    S = (D + 1) * T
    HC = CW // HEAD

    def px(ch, k, d, to):
        cs = pl.ds(ch * CW, CW)
        return remote(pb.at[d, :, :, cs], xr.at[k, :, :, cs], px_s.at[ch, k], px_r.at[ch, k], to, p)

    def parts_each(ch, do):
        for k in range(L, -1, -1):
            if k >= 1:
                @pl.when(even & (c - 2 * k + 1 >= 0))
                def _():
                    do(px(ch, k, 2 * k - 1, c + 1))
            if 2 * k + 1 <= D:
                @pl.when(odd & (c - 2 * k - 1 >= 0))
                def _():
                    do(px(ch, k, 2 * k + 1, c - 1))

    def pz(ch, k):
        cs = pl.ds(ch * CW, CW)
        return remote(zs.at[k, :, :, cs], zr.at[k, :, :, cs], pz_s.at[ch, k], pz_r.at[ch, k], c - 2, p)

    def x_in(ch, k):
        px(ch, k, k, jnp.where(even, c + 1, c - 1)).wait_recv()

    def sum_chain(ch):
        cs = slice(ch * CW, (ch + 1) * CW)
        for k in range(L, -1, -1):
            @pl.when(c - 2 * k >= 0)
            def _():
                @pl.when(odd if 2 * k + 1 > D else (even if k == 0 else c >= 0))
                def _():
                    x_in(ch, k)
                if k + 1 <= L:
                    @pl.when(c + 2 < n)
                    def _():
                        pz(ch, k + 1).wait_recv()
                total = own[:, :, cs] if k == 0 else pb[2 * k, :, :, cs].astype(F32)
                use_x = odd if 2 * k + 1 > D else (even if k == 0 else c >= 0)
                total = total + jnp.where(use_x, xr[k, :, :, cs].astype(F32), 0.0)
                if k + 1 <= L:
                    total = total + jnp.where(c + 2 < n, zr[k + 1, :, :, cs].astype(F32), 0.0)
                if k == 0:
                    own[:, :, cs] = total
                else:
                    zs[k, :, :, cs] = total.astype(BF16)
                    pz(ch, k).start()

    for ch in range(NC):
        if ch + 1 < NC:
            values_up(ch + 1)
        v_chains[ch][1]()

        def head(i, _):
            j = ch * HC + i
            hc = pl.ds(pl.multiple_of(j * HEAD, HEAD), HEAD)
            qa = pl.ds(pl.multiple_of(j * 2 * HEAD, HEAD), HEAD)
            qb = pl.ds(pl.multiple_of(j * 2 * HEAD + HEAD, HEAD), HEAD)
            qh = jnp.concatenate([q_ref[:, qa], q_ref[:, qb]], axis=0)
            gh = jnp.concatenate([g_ref[:, qa], g_ref[:, qb]], axis=0)
            kh = kb[:, :, hc].reshape(S, HEAD)
            vh = vb[:, :, hc].reshape(S, HEAD)
            cr = crow[0:1, :]
            s = mm(kh, qh, 1, 1) * SCALE + bias[...]
            e = jnp.exp(s - jnp.max(s, axis=0, keepdims=True))
            probs = e * (1.0 / jnp.sum(e, axis=0, keepdims=True))
            dp = mm(vh, gh, 1, 1) * cr
            delta = jnp.sum(probs * dp, axis=0, keepdims=True)
            ds = (SCALE * probs * (dp - delta)).astype(BF16)
            wt = (probs * cr).astype(BF16)
            dq = mm(ds, kh, 0, 0).astype(BF16)
            qg_ref[:, qa] = dq[:T]
            qg_ref[:, qb] = dq[T:]
            dk = mm(ds, qh, 1, 0)
            dv = mm(wt, gh, 1, 0)
            own[0, :, hc] = dk[:T]
            own[1, :, hc] = dv[:T]
            pb[1:, 0, :, hc] = dk[T:].astype(BF16).reshape(D, T, HEAD)
            pb[1:, 1, :, hc] = dv[T:].astype(BF16).reshape(D, T, HEAD)
            return 0
        lax.fori_loop(0, HC, head, 0)
        parts_each(ch, lambda copy: copy.start())
        if ch >= 1:
            sum_chain(ch - 1)
    sum_chain(NC - 1)

    kg_ref[...] = own[0].astype(BF16)
    vg = own[1].astype(BF16)
    mid = mm(vg, up_ref[...], 1, 1).astype(BF16)
    uf = ADAPT * mm(lowr[...], vg, 0, 0)
    for h in range(2):
        hu[h] = uf[:, h * HALF:(h + 1) * HALF]
    df = ADAPT * mm(mid, x_ref[...], 0, 0)
    for h in range(2):
        hd[h] = df[:, h * (M // 2):(h + 1) * (M // 2)]

    def both(i, src_d, src_u, dst_d, dst_u, to, pair):
        return (remote(src_d, dst_d, rd_s.at[i], rd_r.at[i], to, pair),
                remote(src_u, dst_u, ru_s.at[i], ru_r.at[i], to, pair))

    tile = 384 if M % 384 == 0 else 128

    def grad_part(j, _):
        t = pl.ds(pl.multiple_of(j * tile, tile), tile)
        g = mm(vg[:, :HALF], wb[0, t, :], 1, 1) + mm(vg[:, HALF:], wb[1, t, :], 1, 1)
        xg_ref[:, t] = (g + ADAPT * mm(mid, dn_ref[t, :], 1, 1)).astype(BF16)
        return 0

    rounds = LOG + 2
    tiles = M // tile
    for i in range(rounds):
        if i <= LOG:
            at_half = 1 - p if i == 0 else p
            hdb[...] = hd[at_half].astype(BF16)
            hub[...] = hu[at_half].astype(BF16)
            if i == 0:
                to, pair = c, 1 - p
            else:
                bit = 1 << (i - 1)
                to, pair = jnp.where(lax.rem(c // bit, 2) == 0, c + bit, c - bit), p
            copies = both(i, hdb, hub, rd.at[i], ru.at[i], to, pair)
        else:
            copies = both(i, hd.at[p], hu.at[p], rfd, rfu, c, 1 - p)
        for copy in copies:
            copy.start()
        lax.fori_loop(tiles * i // rounds, tiles * (i + 1) // rounds, grad_part, 0)
        for copy in copies:
            copy.wait()
        if i <= LOG:
            mine_d = hd[p] if i == 0 else hdb[...].astype(F32)
            mine_u = hu[p] if i == 0 else hub[...].astype(F32)
            hd[p] = mine_d + rd[i].astype(F32)
            hu[p] = mine_u + ru[i].astype(F32)
    dd_ref[p] = hd[p]
    du_ref[p] = hu[p]
    dd_ref[1 - p] = rfd[...]
    du_ref[1 - p] = rfu[...]

    hop(0, c, w_ref.at[p], right).wait_send()
    hop(1, c, w_ref.at[p], left).wait_send()

    def ring_sent(s, _):
        slot = at(pos - s)

        @pl.when(s < NR)
        def _():
            hop(0, slot, block(slot), right).wait_send()
        to_partner(slot).wait_send()

        @pl.when(s <= NL)
        def _():
            slot2 = at(pos + s)

            @pl.when(s < NL)
            def _():
                hop(1, slot2, block(slot2), left).wait_send()
            to_partner(slot2).wait_send()
        return 0
    lax.fori_loop(1, NR + 1, ring_sent, 0)

    def sums_sent(i, _):
        sums(i).wait_send()
        return 0
    lax.fori_loop(1, 2 * n, sums_sent, 0)
    for d in range(1, D + 1):
        @pl.when(c + d < n)
        def _():
            label(d).wait_send()
    k_sent()
    for ch in range(NC):
        v_chains[ch][2]()
        parts_each(ch, lambda copy: copy.wait_send())
        for k in range(1, L + 1):
            @pl.when(c - 2 * k >= 0)
            def _():
                pz(ch, k).wait_send()


def shards(x, q, k, w, dn, up, g, plp, rlp, idx):
    n = lax.axis_size("ctx")
    T, width = k.shape[1], k.shape[2]
    rows = w.shape[0]
    R = -(-rows // 16) * 16
    model = x.shape[2]
    halo = WINDOW // T
    D = min(halo, n - 1)
    L = min(halo // 2, n // 2 - 1)
    NC = 4
    LOG = n.bit_length() - 1
    HALF = width // 2
    pad = R - rows
    M = n * R
    xs = x[0]
    if pad:
        xs = jnp.pad(xs.reshape(T, n, rows), ((0, 0), (0, 0), (0, pad))).reshape(T, M)
    ws = jnp.pad(w.reshape(rows, 2, HALF).transpose(1, 0, 2), ((0, 0), (0, pad), (0, 0)))
    dns = dn
    if pad:
        dns = jnp.pad(dn.reshape(n, rows, dn.shape[1]), ((0, 0), (0, pad), (0, 0))).reshape(M, dn.shape[1])
    lab = jnp.broadcast_to(idx.astype(F32), (SEGS, T))
    gap = jnp.broadcast_to(plp - rlp, (SEGS, T))
    rank = dn.shape[1]
    vm = pl.BlockSpec(memory_space=pltpu.VMEM)
    dma = pltpu.SemaphoreType.DMA
    xg, qg, kg, dd, du = pl.pallas_call(
        functools.partial(kernel, n, L, D, NC, LOG),
        out_shape=(
            jax.ShapeDtypeStruct((T, M), BF16),
            jax.ShapeDtypeStruct(q.shape[1:], BF16),
            jax.ShapeDtypeStruct(k.shape[1:], BF16),
            jax.ShapeDtypeStruct((2, rank, M // 2), F32),
            jax.ShapeDtypeStruct((2, rank, HALF), F32),
        ),
        in_specs=[vm] * 9,
        out_specs=[vm] * 5,
        scratch_shapes=[
            pltpu.VMEM((2, M, HALF), BF16),
            pltpu.VMEM((D + 1, T, width), BF16),
            pltpu.VMEM((D + 1, T, width), BF16),
            pltpu.VMEM((D + 1, SEGS, T), F32),
            pltpu.VMEM((2, n, SEGS, 128), F32),
            pltpu.VMEM(((D + 1) * T, 2 * T), F32),
            pltpu.VMEM((T, rank), BF16),
            pltpu.VMEM((D + 1, 2, T, width), BF16),
            pltpu.VMEM((2, T, width), F32),
            pltpu.VMEM((L + 1, 2, T, width), BF16),
            pltpu.VMEM((L + 1, 2, T, width), BF16),
            pltpu.VMEM((L + 1, 2, T, width), BF16),
            pltpu.VMEM((2, rank, M // 2), F32),
            pltpu.VMEM((2, rank, HALF), F32),
            pltpu.VMEM((rank, M // 2), BF16),
            pltpu.VMEM((rank, HALF), BF16),
            pltpu.VMEM((LOG + 1, rank, M // 2), BF16),
            pltpu.VMEM((LOG + 1, rank, HALF), BF16),
            pltpu.VMEM((rank, M // 2), F32),
            pltpu.VMEM((rank, HALF), F32),
            pltpu.VMEM((8, 2 * T), F32),
            dma((2, n)), dma((n,)), dma((n,)), dma((n,)),
            dma((1, L + 1)), dma((1, L + 1)), dma((1, D + 1)),
            dma((NC, L + 1)), dma((NC, L + 1)), dma((NC, D + 1)),
            dma((D + 1,)), dma((D + 1,)), dma((2 * n,)), dma((2, n)),
            dma((NC, L + 1)), dma((NC, L + 1)), dma((NC, L + 1)), dma((NC, L + 1)),
            dma((LOG + 2,)), dma((LOG + 2,)), dma((LOG + 2,)), dma((LOG + 2,)),
        ],
        compiler_params=pltpu.CompilerParams(
            collective_id=0, has_side_effects=True, vmem_limit_bytes=60 * 1024 * 1024),
    )(xs, q[0], k[0], ws, dns, up, g[0], lab, gap)
    input_grad = xg
    down = dd.transpose(0, 2, 1).reshape(M, rank)
    if pad:
        input_grad = xg.reshape(T, n, R)[:, :, :rows].reshape(T, model)
        down = down.reshape(n, R, rank)[:, :rows].reshape(model, rank)
    upg = du.transpose(1, 0, 2).reshape(rank, width)
    return input_grad[None], qg[None], kg[None], down, upg


def solution(mesh):
    tok = P(("grp", "pair"), "ctx", None)
    row = P(("grp", "pair"), "ctx")
    return jax.shard_map(
        shards,
        mesh=mesh,
        in_specs=(tok, tok, tok, P("ctx", None), P(), P(), tok, row, row, row),
        out_specs=(tok, tok, tok, P("grp", None), P("grp", None)),
        check_vma=False,
    )
```

```python
import functools

import jax
import jax.numpy as jnp
from jax import lax
from jax.experimental import pallas as pl
from jax.experimental.pallas import tpu as pltpu
from jax.sharding import PartitionSpec as P

HEAD = 128
WINDOW = 1024
SEGS = 8
BETA = 0.1
LOSS = 256.0
ADAPT = 2.0
SCALE = 168.0**-0.5
NEG = -1e30
MESH = pl.DeviceIdType.MESH
F32 = jnp.float32
BF16 = jnp.bfloat16


def mm(a, b, ca, cb):
    return lax.dot_general(a, b, (((ca,), (cb,)), ((), ())), preferred_element_type=F32)


def kernel(
    n, L, D, NC, LOG,
    x_ref, q_ref, k_ref, w_ref, dn_ref, up_ref, g_ref, lab_ref, gap_ref,
    xg_ref, qg_ref, kg_ref, dd_ref, du_ref,
    wb, kb, vb, lb, sb, bias, lowr, pb, own, xr, zr, zs,
    hd, hu, hdb, hub, rd, ru, rfd, rfu, crow,
    wring_s, wring_r, wpair_s, wpair_r, wy_s, wy_r, wrest_s, wrest_r,
    kz_s, kx_s, k_r, vz_s, vx_s, v_r, l_s, l_r, s_s, s_r,
    px_s, px_r, pz_s, pz_r, rd_s, rd_r, ru_s, ru_r,
):
    c = lax.axis_index("ctx")
    p = lax.axis_index("pair")
    even = lax.rem(c, 2) == 0
    odd = lax.rem(c, 2) == 1
    T = k_ref.shape[0]
    CW = k_ref.shape[1] // NC
    HALF = k_ref.shape[1] // 2
    M = x_ref.shape[1]
    R = M // n

    y = lax.axis_index("grp")
    U = R * 2 // 7 // 16 * 16

    def block(slot):
        return wb.at[p, pl.ds(pl.multiple_of(slot * R + y * U, 16), R - U), :]

    def across(slot, mine):
        first = (y if mine else 1 - y) * (R - U)
        return wb.at[p, pl.ds(pl.multiple_of(slot * R + first, 16), U), :]

    def to_group(slot):
        return pltpu.make_async_remote_copy(
            src_ref=across(slot, True), dst_ref=across(slot, True), send_sem=wy_s.at[slot], recv_sem=wy_r.at[slot],
            device_id={"grp": 1 - y, "ctx": c, "pair": p}, device_id_type=MESH)

    def group_in(slot):
        return pltpu.make_async_remote_copy(
            src_ref=across(slot, False), dst_ref=across(slot, False), send_sem=wy_s.at[slot], recv_sem=wy_r.at[slot],
            device_id={"grp": 1 - y, "ctx": c, "pair": p}, device_id_type=MESH)

    def rest_to_partner(slot):
        return remote(across(slot, False), across(slot, False), wrest_s.at[slot], wrest_r.at[slot], c, 1 - p)

    def remote(src, dst, ss, rs, ctx, pair):
        return pltpu.make_async_remote_copy(
            src_ref=src, dst_ref=dst, send_sem=ss, recv_sem=rs,
            device_id={"ctx": ctx, "pair": pair}, device_id_type=MESH)

    barrier = pltpu.get_barrier_semaphore()
    me = c * 2 + p

    def greet(i, _):
        other = lax.rem(me + i, 2 * n)
        pl.semaphore_signal(barrier, inc=1, device_id={"ctx": other // 2, "pair": lax.rem(other, 2)},
                            device_id_type=MESH)
        return 0
    lax.fori_loop(1, 2 * n, greet, 0)
    if U:
        pl.semaphore_signal(barrier, inc=1, device_id={"grp": 1 - y, "ctx": c, "pair": p}, device_id_type=MESH)
    pl.semaphore_wait(barrier, 2 * n if U else 2 * n - 1)

    pos = jnp.where(even, c // 2, n - 1 - c // 2)

    def at(position):
        r = lax.rem(position + 2 * n, n)
        return jnp.where(r < n // 2, 2 * r, 2 * (n - 1 - r) + 1)
    right, left = at(pos + 1), at(pos - 1)
    NR = n // 2
    NL = n - 1 - NR

    def hop(direction, slot, src, to):
        return remote(src, block(slot), wring_s.at[direction, slot], wring_r.at[slot], to, p)

    def to_partner(slot):
        return remote(block(slot), block(slot), wpair_s.at[slot], wpair_r.at[slot], c, 1 - p)

    hop(0, c, w_ref.at[p, pl.ds(pl.multiple_of(y * U, 16), R - U), :], right).start()
    hop(1, c, w_ref.at[p, pl.ds(pl.multiple_of(y * U, 16), R - U), :], left).start()

    onehot = (lab_ref[...] == lax.broadcasted_iota(jnp.int32, (SEGS, T), 0).astype(F32)).astype(F32)
    part = jnp.sum(onehot * gap_ref[...], axis=1, keepdims=True)
    sb[p, c] = jnp.broadcast_to(part, (SEGS, 128))
    lb[0] = lab_ref[...]

    def sums(i):
        other = lax.rem(me + i, 2 * n)
        return remote(sb.at[p, c], sb.at[p, c], s_s.at[i], s_r.at[p, c], other // 2, lax.rem(other, 2))

    def send_sums(i, _):
        sums(i).start()
        return 0
    lax.fori_loop(1, 2 * n, send_sums, 0)

    def label(d):
        return remote(lb.at[0], lb.at[d], l_s.at[d], l_r.at[d], c + d, p)
    for d in range(1, D + 1):
        @pl.when(c + d < n)
        def _():
            label(d).start()

        @pl.when(c - d < 0)
        def _():
            kb[d] = jnp.zeros_like(kb[d])
            vb[d] = jnp.zeros_like(vb[d])
            lb[d] = jnp.full_like(lb[d], -1.0)

    def chain(buf, zs_, xs_, rs_, src, cols, ch):
        def cut(ref):
            return ref if cols is None else ref.at[:, cols]

        def z(k):
            return remote(cut(src if k == 0 else buf.at[2 * k]), cut(buf.at[2 * k + 2]), zs_.at[ch, k],
                          rs_.at[ch, 2 * k + 2], c + 2, p)

        def xe(k):
            return remote(cut(src if k == 0 else buf.at[2 * k]), cut(buf.at[2 * k + 1]), xs_.at[ch, k],
                          rs_.at[ch, 2 * k + 1], c + 1, p)

        def xo(k):
            return remote(cut(buf.at[2 * k]), cut(buf.at[2 * k - 1]), xs_.at[ch, k], rs_.at[ch, 2 * k - 1], c - 1, p)

        def each(k, do):
            if k < L:
                @pl.when((c + 2 < n) & (c - 2 * k >= 0))
                def _():
                    do(z(k))
            if 2 * k + 1 <= D:
                @pl.when(even & (c - 2 * k >= 0))
                def _():
                    do(xe(k))
            if k >= 1:
                @pl.when(odd & (c - 2 * k >= 0))
                def _():
                    do(xo(k))

        def arrived(d):
            @pl.when(c - d >= 0)
            def _():
                remote(cut(buf.at[d]), cut(buf.at[d]), zs_.at[ch, 0], rs_.at[ch, d], c - d, p).wait_recv()

        def step(k):
            if k >= 1:
                arrived(2 * k)
            each(k, lambda copy: copy.start())

        def rest():
            for d in range(1, D + 1, 2):
                arrived(d)

        def sent():
            for k in range(L + 1):
                each(k, lambda copy: copy.wait_send())
        return step, rest, sent

    k_step, k_rest, k_sent = chain(kb, kz_s, kx_s, k_r, k_ref, None, 0)
    k_step(0)
    kb[0] = k_ref[...]
    for h in range(2):
        wb[h, pl.ds(pl.multiple_of(c * R, 16), R), :] = w_ref[h]

    lowr[...] = mm(x_ref[...], dn_ref[...], 1, 0).astype(BF16)

    def ring_step(s):
        slot = at(pos - s)
        hop(0, slot, block(slot), right).wait_recv()

        @pl.when(s < NR)
        def _():
            hop(0, slot, block(slot), right).start()
        to_partner(slot).start()
        if U:
            to_group(slot).start()

        @pl.when(s <= NL)
        def _():
            slot2 = at(pos + s)
            hop(1, slot2, block(slot2), left).wait_recv()

            @pl.when(s < NL)
            def _():
                hop(1, slot2, block(slot2), left).start()
            to_partner(slot2).start()
            if U:
                to_group(slot2).start()

    if n <= 16:
        for s in range(1, NR + 1):
            ring_step(jnp.int32(s))
            if s <= L:
                k_step(s)
        for s in range(NR + 1, L + 1):
            k_step(s)
    else:
        def ring_body(s, _):
            ring_step(s)
            return 0
        lax.fori_loop(1, NR + 1, ring_body, 0)
        for s in range(1, L + 1):
            k_step(s)

    if U:
        def group_arrived(s, _):
            slot = at(pos - s)
            group_in(slot).wait_recv()
            rest_to_partner(slot).start()

            @pl.when(s <= NL)
            def _():
                slot2 = at(pos + s)
                group_in(slot2).wait_recv()
                rest_to_partner(slot2).start()
            return 0
        lax.fori_loop(1, NR + 1, group_arrived, 0)

    def partner_rows(slot):
        return wb.at[1 - p, pl.ds(pl.multiple_of(slot * R + y * U, 16), R - U), :]

    def partner_rest(slot):
        return wb.at[1 - p, pl.ds(pl.multiple_of(slot * R + (1 - y) * (R - U), 16), U), :]

    def partner_in(i, _):
        slot = lax.rem(c + i, n)
        rows = partner_rows(slot)
        remote(rows, rows, wpair_s.at[slot], wpair_r.at[slot], c, 1 - p).wait_recv()
        if U:
            more = partner_rest(slot)
            remote(more, more, wrest_s.at[slot], wrest_r.at[slot], c, 1 - p).wait_recv()
        return 0
    lax.fori_loop(1, n, partner_in, 0)

    v_chains = []
    for ch in range(NC):
        lo = ch * CW
        cols = slice(lo, lo + CW)
        half, inner = lo // HALF, lo % HALF

        acc = mm(x_ref[...], wb[half, :, inner:inner + CW], 1, 0) + ADAPT * mm(lowr[...], up_ref[:, cols], 1, 0)
        vb[0, :, cols] = acc.astype(BF16)
        steps = chain(vb, vz_s, vx_s, v_r, vb.at[0], pl.ds(lo, CW), ch)
        v_chains.append(steps)
        steps[0](0)

    def sums_in(i, _):
        other = lax.rem(me + i, 2 * n)
        remote(sb.at[0, 0], sb.at[lax.rem(other, 2), other // 2], s_s.at[i], s_r.at[lax.rem(other, 2), other // 2],
               other // 2, lax.rem(other, 2)).wait_recv()
        return 0
    lax.fori_loop(1, 2 * n, sums_in, 0)
    margin = BETA * (jnp.sum(sb[0], axis=0) - jnp.sum(sb[1], axis=0))
    sign = 2.0 * p.astype(F32) - 1.0
    coef = sign * (BETA * LOSS) * jax.nn.sigmoid(-margin)
    token_coef = jnp.sum(onehot * coef, axis=0, keepdims=True)
    crow[...] = jnp.broadcast_to(jnp.concatenate([token_coef, token_coef], axis=1), crow.shape)

    lq = lab_ref[0:1, :]
    for d in range(D + 1):
        if d:
            @pl.when(c - d >= 0)
            def _():
                remote(lb.at[d], lb.at[d], l_s.at[d], l_r.at[d], c - d, p).wait_recv()
        lk = jnp.transpose(jnp.broadcast_to(lb[d][0:1, :], (T, T)))
        apart = (d * T + lax.broadcasted_iota(jnp.int32, (T, T), 1) - lax.broadcasted_iota(jnp.int32, (T, T), 0))
        ok = (lk == lq) & (apart >= 0) & (apart < WINDOW)
        b = jnp.where(ok, 0.0, NEG)
        bias[d * T:(d + 1) * T, :] = jnp.concatenate([b, b], axis=1)

    def values_up(ch):
        for k in range(1, L + 1):
            v_chains[ch][0](k)

    values_up(0)
    k_rest()

    S = (D + 1) * T
    HC = CW // HEAD

    def px(ch, k, d, to):
        cs = pl.ds(ch * CW, CW)
        return remote(pb.at[d, :, :, cs], xr.at[k, :, :, cs], px_s.at[ch, k], px_r.at[ch, k], to, p)

    def parts_each(ch, do):
        for k in range(L, -1, -1):
            if k >= 1:
                @pl.when(even & (c - 2 * k + 1 >= 0))
                def _():
                    do(px(ch, k, 2 * k - 1, c + 1))
            if 2 * k + 1 <= D:
                @pl.when(odd & (c - 2 * k - 1 >= 0))
                def _():
                    do(px(ch, k, 2 * k + 1, c - 1))

    def pz(ch, k):
        cs = pl.ds(ch * CW, CW)
        return remote(zs.at[k, :, :, cs], zr.at[k, :, :, cs], pz_s.at[ch, k], pz_r.at[ch, k], c - 2, p)

    def x_in(ch, k):
        px(ch, k, k, jnp.where(even, c + 1, c - 1)).wait_recv()

    def sum_chain(ch):
        cs = slice(ch * CW, (ch + 1) * CW)
        for k in range(L, -1, -1):
            @pl.when(c - 2 * k >= 0)
            def _():
                @pl.when(odd if 2 * k + 1 > D else (even if k == 0 else c >= 0))
                def _():
                    x_in(ch, k)
                if k + 1 <= L:
                    @pl.when(c + 2 < n)
                    def _():
                        pz(ch, k + 1).wait_recv()
                total = own[:, :, cs] if k == 0 else pb[2 * k, :, :, cs].astype(F32)
                use_x = odd if 2 * k + 1 > D else (even if k == 0 else c >= 0)
                total = total + jnp.where(use_x, xr[k, :, :, cs].astype(F32), 0.0)
                if k + 1 <= L:
                    total = total + jnp.where(c + 2 < n, zr[k + 1, :, :, cs].astype(F32), 0.0)
                if k == 0:
                    own[:, :, cs] = total
                else:
                    zs[k, :, :, cs] = total.astype(BF16)
                    pz(ch, k).start()

    for ch in range(NC):
        if ch + 1 < NC:
            values_up(ch + 1)
        v_chains[ch][1]()

        def head(i, _):
            j = ch * HC + i
            hc = pl.ds(pl.multiple_of(j * HEAD, HEAD), HEAD)
            qa = pl.ds(pl.multiple_of(j * 2 * HEAD, HEAD), HEAD)
            qb = pl.ds(pl.multiple_of(j * 2 * HEAD + HEAD, HEAD), HEAD)
            qh = jnp.concatenate([q_ref[:, qa], q_ref[:, qb]], axis=0)
            gh = jnp.concatenate([g_ref[:, qa], g_ref[:, qb]], axis=0)
            kh = kb[:, :, hc].reshape(S, HEAD)
            vh = vb[:, :, hc].reshape(S, HEAD)
            cr = crow[0:1, :]
            s = mm(kh, qh, 1, 1) * SCALE + bias[...]
            e = jnp.exp(s - jnp.max(s, axis=0, keepdims=True))
            probs = e * (1.0 / jnp.sum(e, axis=0, keepdims=True))
            dp = mm(vh, gh, 1, 1) * cr
            delta = jnp.sum(probs * dp, axis=0, keepdims=True)
            ds = (SCALE * probs * (dp - delta)).astype(BF16)
            wt = (probs * cr).astype(BF16)
            dq = mm(ds, kh, 0, 0).astype(BF16)
            qg_ref[:, qa] = dq[:T]
            qg_ref[:, qb] = dq[T:]
            dk = mm(ds, qh, 1, 0)
            dv = mm(wt, gh, 1, 0)
            own[0, :, hc] = dk[:T]
            own[1, :, hc] = dv[:T]
            pb[1:, 0, :, hc] = dk[T:].astype(BF16).reshape(D, T, HEAD)
            pb[1:, 1, :, hc] = dv[T:].astype(BF16).reshape(D, T, HEAD)
            return 0
        lax.fori_loop(0, HC, head, 0)
        parts_each(ch, lambda copy: copy.start())
        if ch >= 1:
            sum_chain(ch - 1)
    sum_chain(NC - 1)

    kg_ref[...] = own[0].astype(BF16)
    vg = own[1].astype(BF16)
    mid = mm(vg, up_ref[...], 1, 1).astype(BF16)
    uf = ADAPT * mm(lowr[...], vg, 0, 0)
    for h in range(2):
        hu[h] = uf[:, h * HALF:(h + 1) * HALF]
    df = ADAPT * mm(mid, x_ref[...], 0, 0)
    for h in range(2):
        hd[h] = df[:, h * (M // 2):(h + 1) * (M // 2)]

    def both(i, src_d, src_u, dst_d, dst_u, to, pair):
        return (remote(src_d, dst_d, rd_s.at[i], rd_r.at[i], to, pair),
                remote(src_u, dst_u, ru_s.at[i], ru_r.at[i], to, pair))

    tile = 384 if M % 384 == 0 else 128

    def grad_part(j, _):
        t = pl.ds(pl.multiple_of(j * tile, tile), tile)
        g = mm(vg[:, :HALF], wb[0, t, :], 1, 1) + mm(vg[:, HALF:], wb[1, t, :], 1, 1)
        xg_ref[:, t] = (g + ADAPT * mm(mid, dn_ref[t, :], 1, 1)).astype(BF16)
        return 0

    rounds = LOG + 2
    tiles = M // tile
    for i in range(rounds):
        if i <= LOG:
            at_half = 1 - p if i == 0 else p
            hdb[...] = hd[at_half].astype(BF16)
            hub[...] = hu[at_half].astype(BF16)
            if i == 0:
                to, pair = c, 1 - p
            else:
                bit = 1 << (i - 1)
                to, pair = jnp.where(lax.rem(c // bit, 2) == 0, c + bit, c - bit), p
            copies = both(i, hdb, hub, rd.at[i], ru.at[i], to, pair)
        else:
            copies = both(i, hd.at[p], hu.at[p], rfd, rfu, c, 1 - p)
        for copy in copies:
            copy.start()
        lax.fori_loop(tiles * i // rounds, tiles * (i + 1) // rounds, grad_part, 0)
        for copy in copies:
            copy.wait()
        if i <= LOG:
            mine_d = hd[p] if i == 0 else hdb[...].astype(F32)
            mine_u = hu[p] if i == 0 else hub[...].astype(F32)
            hd[p] = mine_d + rd[i].astype(F32)
            hu[p] = mine_u + ru[i].astype(F32)
    dd_ref[p] = hd[p]
    du_ref[p] = hu[p]
    dd_ref[1 - p] = rfd[...]
    du_ref[1 - p] = rfu[...]

    hop(0, c, w_ref.at[p, pl.ds(pl.multiple_of(y * U, 16), R - U), :], right).wait_send()
    hop(1, c, w_ref.at[p, pl.ds(pl.multiple_of(y * U, 16), R - U), :], left).wait_send()

    def ring_sent(s, _):
        slot = at(pos - s)

        @pl.when(s < NR)
        def _():
            hop(0, slot, block(slot), right).wait_send()
        to_partner(slot).wait_send()
        if U:
            to_group(slot).wait_send()
            rest_to_partner(slot).wait_send()

        @pl.when(s <= NL)
        def _():
            slot2 = at(pos + s)

            @pl.when(s < NL)
            def _():
                hop(1, slot2, block(slot2), left).wait_send()
            to_partner(slot2).wait_send()
            if U:
                to_group(slot2).wait_send()
                rest_to_partner(slot2).wait_send()
        return 0
    lax.fori_loop(1, NR + 1, ring_sent, 0)

    def sums_sent(i, _):
        sums(i).wait_send()
        return 0
    lax.fori_loop(1, 2 * n, sums_sent, 0)
    for d in range(1, D + 1):
        @pl.when(c + d < n)
        def _():
            label(d).wait_send()
    k_sent()
    for ch in range(NC):
        v_chains[ch][2]()
        parts_each(ch, lambda copy: copy.wait_send())
        for k in range(1, L + 1):
            @pl.when(c - 2 * k >= 0)
            def _():
                pz(ch, k).wait_send()


def shards(x, q, k, w, dn, up, g, plp, rlp, idx):
    n = lax.axis_size("ctx")
    T, width = k.shape[1], k.shape[2]
    rows = w.shape[0]
    R = -(-rows // 16) * 16
    model = x.shape[2]
    halo = WINDOW // T
    D = min(halo, n - 1)
    L = min(halo // 2, n // 2 - 1)
    NC = 4
    LOG = n.bit_length() - 1
    HALF = width // 2
    pad = R - rows
    M = n * R
    xs = x[0]
    if pad:
        xs = jnp.pad(xs.reshape(T, n, rows), ((0, 0), (0, 0), (0, pad))).reshape(T, M)
    ws = jnp.pad(w.reshape(rows, 2, HALF).transpose(1, 0, 2), ((0, 0), (0, pad), (0, 0)))
    dns = dn
    if pad:
        dns = jnp.pad(dn.reshape(n, rows, dn.shape[1]), ((0, 0), (0, pad), (0, 0))).reshape(M, dn.shape[1])
    lab = jnp.broadcast_to(idx.astype(F32), (SEGS, T))
    gap = jnp.broadcast_to(plp - rlp, (SEGS, T))
    rank = dn.shape[1]
    vm = pl.BlockSpec(memory_space=pltpu.VMEM)
    dma = pltpu.SemaphoreType.DMA
    xg, qg, kg, dd, du = pl.pallas_call(
        functools.partial(kernel, n, L, D, NC, LOG),
        out_shape=(
            jax.ShapeDtypeStruct((T, M), BF16),
            jax.ShapeDtypeStruct(q.shape[1:], BF16),
            jax.ShapeDtypeStruct(k.shape[1:], BF16),
            jax.ShapeDtypeStruct((2, rank, M // 2), F32),
            jax.ShapeDtypeStruct((2, rank, HALF), F32),
        ),
        in_specs=[vm] * 9,
        out_specs=[vm] * 5,
        scratch_shapes=[
            pltpu.VMEM((2, M, HALF), BF16),
            pltpu.VMEM((D + 1, T, width), BF16),
            pltpu.VMEM((D + 1, T, width), BF16),
            pltpu.VMEM((D + 1, SEGS, T), F32),
            pltpu.VMEM((2, n, SEGS, 128), F32),
            pltpu.VMEM(((D + 1) * T, 2 * T), F32),
            pltpu.VMEM((T, rank), BF16),
            pltpu.VMEM((D + 1, 2, T, width), BF16),
            pltpu.VMEM((2, T, width), F32),
            pltpu.VMEM((L + 1, 2, T, width), BF16),
            pltpu.VMEM((L + 1, 2, T, width), BF16),
            pltpu.VMEM((L + 1, 2, T, width), BF16),
            pltpu.VMEM((2, rank, M // 2), F32),
            pltpu.VMEM((2, rank, HALF), F32),
            pltpu.VMEM((rank, M // 2), BF16),
            pltpu.VMEM((rank, HALF), BF16),
            pltpu.VMEM((LOG + 1, rank, M // 2), BF16),
            pltpu.VMEM((LOG + 1, rank, HALF), BF16),
            pltpu.VMEM((rank, M // 2), F32),
            pltpu.VMEM((rank, HALF), F32),
            pltpu.VMEM((8, 2 * T), F32),
            dma((2, n)), dma((n,)), dma((n,)), dma((n,)), dma((n,)), dma((n,)), dma((n,)), dma((n,)),
            dma((1, L + 1)), dma((1, L + 1)), dma((1, D + 1)),
            dma((NC, L + 1)), dma((NC, L + 1)), dma((NC, D + 1)),
            dma((D + 1,)), dma((D + 1,)), dma((2 * n,)), dma((2, n)),
            dma((NC, L + 1)), dma((NC, L + 1)), dma((NC, L + 1)), dma((NC, L + 1)),
            dma((LOG + 2,)), dma((LOG + 2,)), dma((LOG + 2,)), dma((LOG + 2,)),
        ],
        compiler_params=pltpu.CompilerParams(
            collective_id=0, has_side_effects=True, vmem_limit_bytes=60 * 1024 * 1024),
    )(xs, q[0], k[0], ws, dns, up, g[0], lab, gap)
    input_grad = xg
    down = dd.transpose(0, 2, 1).reshape(M, rank)
    if pad:
        input_grad = xg.reshape(T, n, R)[:, :, :rows].reshape(T, model)
        down = down.reshape(n, R, rank)[:, :rows].reshape(model, rank)
    upg = du.transpose(1, 0, 2).reshape(rank, width)
    return input_grad[None], qg[None], kg[None], down, upg


def solution(mesh):
    tok = P(("grp", "pair"), "ctx", None)
    row = P(("grp", "pair"), "ctx")
    return jax.shard_map(
        shards,
        mesh=mesh,
        in_specs=(tok, tok, tok, P("ctx", None), P(), P(), tok, row, row, row),
        out_specs=(tok, tok, tok, P("grp", None), P("grp", None)),
        check_vma=False,
    )
```

```python
import functools

import jax
import jax.numpy as jnp
from jax import lax
from jax.experimental import pallas as pl
from jax.experimental.pallas import tpu as pltpu
from jax.sharding import PartitionSpec as P

HEAD = 128
WINDOW = 1024
SEGS = 8
BETA = 0.1
LOSS = 256.0
ADAPT = 2.0
SCALE = 168.0**-0.5
NEG = -1e30
MESH = pl.DeviceIdType.MESH
F32 = jnp.float32
BF16 = jnp.bfloat16


def mm(a, b, ca, cb):
    return lax.dot_general(a, b, (((ca,), (cb,)), ((), ())), preferred_element_type=F32)


def kernel(
    n, L, D, NC, LOG,
    x_ref, q_ref, k_ref, w_ref, dn_ref, up_ref, g_ref, lab_ref, gap_ref,
    xg_ref, qg_ref, kg_ref, dd_ref, du_ref,
    wb, kb, vb, lb, sb, bias, lowr, pb, own, xr, zr, zs,
    hd, hu, hdb, hub, rd, ru, rfd, rfu, crow,
    wring_s, wring_r, wpair_s, wpair_r, wy_s, wy_r, wrest_s, wrest_r,
    kz_s, kx_s, k_r, vz_s, vx_s, v_r, l_s, l_r, s_s, s_r,
    px_s, px_r, pz_s, pz_r, rd_s, rd_r, ru_s, ru_r,
):
    c = lax.axis_index("ctx")
    p = lax.axis_index("pair")
    even = lax.rem(c, 2) == 0
    odd = lax.rem(c, 2) == 1
    T = k_ref.shape[0]
    CW = k_ref.shape[1] // NC
    HALF = k_ref.shape[1] // 2
    M = x_ref.shape[1]
    R = M // n

    y = lax.axis_index("grp")
    U = R * 2 // 7 // 16 * 16

    def block(slot):
        return wb.at[p, pl.ds(pl.multiple_of(slot * R + y * U, 16), R - U), :]

    def across(slot, mine):
        first = (y if mine else 1 - y) * (R - U)
        return wb.at[p, pl.ds(pl.multiple_of(slot * R + first, 16), U), :]

    def to_group(slot):
        return pltpu.make_async_remote_copy(
            src_ref=across(slot, True), dst_ref=across(slot, True), send_sem=wy_s.at[slot], recv_sem=wy_r.at[slot],
            device_id={"grp": 1 - y, "ctx": c, "pair": p}, device_id_type=MESH)

    def group_in(slot):
        return pltpu.make_async_remote_copy(
            src_ref=across(slot, False), dst_ref=across(slot, False), send_sem=wy_s.at[slot], recv_sem=wy_r.at[slot],
            device_id={"grp": 1 - y, "ctx": c, "pair": p}, device_id_type=MESH)

    def rest_to_partner(slot):
        return remote(across(slot, False), across(slot, False), wrest_s.at[slot], wrest_r.at[slot], c, 1 - p)

    def remote(src, dst, ss, rs, ctx, pair):
        return pltpu.make_async_remote_copy(
            src_ref=src, dst_ref=dst, send_sem=ss, recv_sem=rs,
            device_id={"ctx": ctx, "pair": pair}, device_id_type=MESH)

    barrier = pltpu.get_barrier_semaphore()
    me = c * 2 + p

    def greet(i, _):
        other = lax.rem(me + i, 2 * n)
        pl.semaphore_signal(barrier, inc=1, device_id={"ctx": other // 2, "pair": lax.rem(other, 2)},
                            device_id_type=MESH)
        return 0
    lax.fori_loop(1, 2 * n, greet, 0)
    if U:
        pl.semaphore_signal(barrier, inc=1, device_id={"grp": 1 - y, "ctx": c, "pair": p}, device_id_type=MESH)
    pl.semaphore_wait(barrier, 2 * n if U else 2 * n - 1)

    pos = jnp.where(even, c // 2, n - 1 - c // 2)

    def at(position):
        r = lax.rem(position + 2 * n, n)
        return jnp.where(r < n // 2, 2 * r, 2 * (n - 1 - r) + 1)
    right, left = at(pos + 1), at(pos - 1)
    NR = n // 2
    NL = n - 1 - NR

    def hop(direction, slot, src, to):
        return remote(src, block(slot), wring_s.at[direction, slot], wring_r.at[slot], to, p)

    def to_partner(slot):
        return remote(block(slot), block(slot), wpair_s.at[slot], wpair_r.at[slot], c, 1 - p)

    hop(0, c, w_ref.at[p, pl.ds(pl.multiple_of(y * U, 16), R - U), :], right).start()
    hop(1, c, w_ref.at[p, pl.ds(pl.multiple_of(y * U, 16), R - U), :], left).start()

    onehot = (lab_ref[...] == lax.broadcasted_iota(jnp.int32, (SEGS, T), 0).astype(F32)).astype(F32)
    part = jnp.sum(onehot * gap_ref[...], axis=1, keepdims=True)
    sb[p, c] = jnp.broadcast_to(part, (SEGS, 128))
    lb[0] = lab_ref[...]

    def sums(i):
        other = lax.rem(me + i, 2 * n)
        return remote(sb.at[p, c], sb.at[p, c], s_s.at[i], s_r.at[p, c], other // 2, lax.rem(other, 2))

    def send_sums(i, _):
        sums(i).start()
        return 0
    lax.fori_loop(1, 2 * n, send_sums, 0)

    def label(d):
        return remote(lb.at[0], lb.at[d], l_s.at[d], l_r.at[d], c + d, p)
    for d in range(1, D + 1):
        @pl.when(c + d < n)
        def _():
            label(d).start()

        @pl.when(c - d < 0)
        def _():
            kb[d] = jnp.zeros_like(kb[d])
            vb[d] = jnp.zeros_like(vb[d])
            lb[d] = jnp.full_like(lb[d], -1.0)

    def chain(buf, zs_, xs_, rs_, src, cols, ch):
        def cut(ref):
            return ref if cols is None else ref.at[:, cols]

        def z(k):
            return remote(cut(src if k == 0 else buf.at[2 * k]), cut(buf.at[2 * k + 2]), zs_.at[ch, k],
                          rs_.at[ch, 2 * k + 2], c + 2, p)

        def xe(k):
            return remote(cut(src if k == 0 else buf.at[2 * k]), cut(buf.at[2 * k + 1]), xs_.at[ch, k],
                          rs_.at[ch, 2 * k + 1], c + 1, p)

        def xo(k):
            return remote(cut(buf.at[2 * k]), cut(buf.at[2 * k - 1]), xs_.at[ch, k], rs_.at[ch, 2 * k - 1], c - 1, p)

        def each(k, do):
            if k < L:
                @pl.when((c + 2 < n) & (c - 2 * k >= 0))
                def _():
                    do(z(k))
            if 2 * k + 1 <= D:
                @pl.when(even & (c - 2 * k >= 0))
                def _():
                    do(xe(k))
            if k >= 1:
                @pl.when(odd & (c - 2 * k >= 0))
                def _():
                    do(xo(k))

        def arrived(d):
            @pl.when(c - d >= 0)
            def _():
                remote(cut(buf.at[d]), cut(buf.at[d]), zs_.at[ch, 0], rs_.at[ch, d], c - d, p).wait_recv()

        def step(k):
            if k >= 1:
                arrived(2 * k)
            each(k, lambda copy: copy.start())

        def rest():
            for d in range(1, D + 1, 2):
                arrived(d)

        def sent():
            for k in range(L + 1):
                each(k, lambda copy: copy.wait_send())
        return step, rest, sent

    k_step, k_rest, k_sent = chain(kb, kz_s, kx_s, k_r, k_ref, None, 0)
    k_step(0)
    kb[0] = k_ref[...]
    for h in range(2):
        wb[h, pl.ds(pl.multiple_of(c * R, 16), R), :] = w_ref[h]

    lowr[...] = mm(x_ref[...], dn_ref[...], 1, 0).astype(BF16)

    def ring_step(s):
        slot = at(pos - s)
        hop(0, slot, block(slot), right).wait_recv()

        @pl.when(s < NR)
        def _():
            hop(0, slot, block(slot), right).start()
        to_partner(slot).start()
        if U:
            to_group(slot).start()

        @pl.when(s <= NL)
        def _():
            slot2 = at(pos + s)
            hop(1, slot2, block(slot2), left).wait_recv()

            @pl.when(s < NL)
            def _():
                hop(1, slot2, block(slot2), left).start()
            to_partner(slot2).start()
            if U:
                to_group(slot2).start()

    if n <= 16:
        for s in range(1, NR + 1):
            ring_step(jnp.int32(s))
            if s <= L:
                k_step(s)
        for s in range(NR + 1, L + 1):
            k_step(s)
    else:
        def ring_body(s, _):
            ring_step(s)
            return 0
        lax.fori_loop(1, NR + 1, ring_body, 0)
        for s in range(1, L + 1):
            k_step(s)

    if U:
        def group_arrived(s, _):
            slot = at(pos - s)
            group_in(slot).wait_recv()
            rest_to_partner(slot).start()

            @pl.when(s <= NL)
            def _():
                slot2 = at(pos + s)
                group_in(slot2).wait_recv()
                rest_to_partner(slot2).start()
            return 0
        lax.fori_loop(1, NR + 1, group_arrived, 0)

    def partner_rows(slot):
        return wb.at[1 - p, pl.ds(pl.multiple_of(slot * R + y * U, 16), R - U), :]

    def partner_rest(slot):
        return wb.at[1 - p, pl.ds(pl.multiple_of(slot * R + (1 - y) * (R - U), 16), U), :]

    def partner_in(i, _):
        slot = lax.rem(c + i, n)
        rows = partner_rows(slot)
        remote(rows, rows, wpair_s.at[slot], wpair_r.at[slot], c, 1 - p).wait_recv()
        if U:
            more = partner_rest(slot)
            remote(more, more, wrest_s.at[slot], wrest_r.at[slot], c, 1 - p).wait_recv()
        return 0
    lax.fori_loop(1, n, partner_in, 0)

    v_chains = []
    for ch in range(NC):
        lo = ch * CW
        cols = slice(lo, lo + CW)
        half, inner = lo // HALF, lo % HALF

        if ch % 2 == 0:
            wide = slice(lo, lo + 2 * CW)
            acc = mm(x_ref[...], wb[half, :, inner:inner + 2 * CW], 1, 0) + ADAPT * mm(lowr[...], up_ref[:, wide], 1, 0)
            vb[0, :, wide] = acc.astype(BF16)
        steps = chain(vb, vz_s, vx_s, v_r, vb.at[0], pl.ds(lo, CW), ch)
        v_chains.append(steps)
        steps[0](0)

    def sums_in(i, _):
        other = lax.rem(me + i, 2 * n)
        remote(sb.at[0, 0], sb.at[lax.rem(other, 2), other // 2], s_s.at[i], s_r.at[lax.rem(other, 2), other // 2],
               other // 2, lax.rem(other, 2)).wait_recv()
        return 0
    lax.fori_loop(1, 2 * n, sums_in, 0)
    margin = BETA * (jnp.sum(sb[0], axis=0) - jnp.sum(sb[1], axis=0))
    sign = 2.0 * p.astype(F32) - 1.0
    coef = sign * (BETA * LOSS) * jax.nn.sigmoid(-margin)
    token_coef = jnp.sum(onehot * coef, axis=0, keepdims=True)
    crow[...] = jnp.broadcast_to(jnp.concatenate([token_coef, token_coef], axis=1), crow.shape)

    lq = lab_ref[0:1, :]
    for d in range(D + 1):
        if d:
            @pl.when(c - d >= 0)
            def _():
                remote(lb.at[d], lb.at[d], l_s.at[d], l_r.at[d], c - d, p).wait_recv()
        lk = jnp.transpose(jnp.broadcast_to(lb[d][0:1, :], (T, T)))
        apart = (d * T + lax.broadcasted_iota(jnp.int32, (T, T), 1) - lax.broadcasted_iota(jnp.int32, (T, T), 0))
        ok = (lk == lq) & (apart >= 0) & (apart < WINDOW)
        b = jnp.where(ok, 0.0, NEG)
        bias[d * T:(d + 1) * T, :] = jnp.concatenate([b, b], axis=1)

    def values_up(ch):
        for k in range(1, L + 1):
            v_chains[ch][0](k)

    values_up(0)
    k_rest()

    S = (D + 1) * T
    HC = CW // HEAD

    def px(ch, k, d, to):
        cs = pl.ds(ch * CW, CW)
        return remote(pb.at[d, :, :, cs], xr.at[k, :, :, cs], px_s.at[ch, k], px_r.at[ch, k], to, p)

    def parts_each(ch, do):
        for k in range(L, -1, -1):
            if k >= 1:
                @pl.when(even & (c - 2 * k + 1 >= 0))
                def _():
                    do(px(ch, k, 2 * k - 1, c + 1))
            if 2 * k + 1 <= D:
                @pl.when(odd & (c - 2 * k - 1 >= 0))
                def _():
                    do(px(ch, k, 2 * k + 1, c - 1))

    def pz(ch, k):
        cs = pl.ds(ch * CW, CW)
        return remote(zs.at[k, :, :, cs], zr.at[k, :, :, cs], pz_s.at[ch, k], pz_r.at[ch, k], c - 2, p)

    def x_in(ch, k):
        px(ch, k, k, jnp.where(even, c + 1, c - 1)).wait_recv()

    def sum_chain(ch):
        cs = slice(ch * CW, (ch + 1) * CW)
        for k in range(L, -1, -1):
            @pl.when(c - 2 * k >= 0)
            def _():
                @pl.when(odd if 2 * k + 1 > D else (even if k == 0 else c >= 0))
                def _():
                    x_in(ch, k)
                if k + 1 <= L:
                    @pl.when(c + 2 < n)
                    def _():
                        pz(ch, k + 1).wait_recv()
                total = own[:, :, cs] if k == 0 else pb[2 * k, :, :, cs].astype(F32)
                use_x = odd if 2 * k + 1 > D else (even if k == 0 else c >= 0)
                total = total + jnp.where(use_x, xr[k, :, :, cs].astype(F32), 0.0)
                if k + 1 <= L:
                    total = total + jnp.where(c + 2 < n, zr[k + 1, :, :, cs].astype(F32), 0.0)
                if k == 0:
                    own[:, :, cs] = total
                else:
                    zs[k, :, :, cs] = total.astype(BF16)
                    pz(ch, k).start()

    for ch in range(NC):
        if ch + 1 < NC:
            values_up(ch + 1)
        v_chains[ch][1]()

        def head(i, _):
            j = ch * HC + i
            hc = pl.ds(pl.multiple_of(j * HEAD, HEAD), HEAD)
            qa = pl.ds(pl.multiple_of(j * 2 * HEAD, HEAD), HEAD)
            qb = pl.ds(pl.multiple_of(j * 2 * HEAD + HEAD, HEAD), HEAD)
            qh = jnp.concatenate([q_ref[:, qa], q_ref[:, qb]], axis=0)
            gh = jnp.concatenate([g_ref[:, qa], g_ref[:, qb]], axis=0)
            kh = kb[:, :, hc].reshape(S, HEAD)
            vh = vb[:, :, hc].reshape(S, HEAD)
            cr = crow[0:1, :]
            s = mm(kh, qh, 1, 1) * SCALE + bias[...]
            e = jnp.exp(s - jnp.max(s, axis=0, keepdims=True))
            probs = e * (1.0 / jnp.sum(e, axis=0, keepdims=True))
            dp = mm(vh, gh, 1, 1) * cr
            delta = jnp.sum(probs * dp, axis=0, keepdims=True)
            ds = (SCALE * probs * (dp - delta)).astype(BF16)
            wt = (probs * cr).astype(BF16)
            dq = mm(ds, kh, 0, 0).astype(BF16)
            qg_ref[:, qa] = dq[:T]
            qg_ref[:, qb] = dq[T:]
            dk = mm(ds, qh, 1, 0)
            dv = mm(wt, gh, 1, 0)
            own[0, :, hc] = dk[:T]
            own[1, :, hc] = dv[:T]
            pb[1:, 0, :, hc] = dk[T:].astype(BF16).reshape(D, T, HEAD)
            pb[1:, 1, :, hc] = dv[T:].astype(BF16).reshape(D, T, HEAD)
            return 0
        lax.fori_loop(0, HC, head, 0)
        parts_each(ch, lambda copy: copy.start())
        if ch >= 1:
            sum_chain(ch - 1)
    sum_chain(NC - 1)

    kg_ref[...] = own[0].astype(BF16)
    vg = own[1].astype(BF16)
    mid = mm(vg, up_ref[...], 1, 1).astype(BF16)
    uf = ADAPT * mm(lowr[...], vg, 0, 0)
    for h in range(2):
        hu[h] = uf[:, h * HALF:(h + 1) * HALF]
    df = ADAPT * mm(mid, x_ref[...], 0, 0)
    for h in range(2):
        hd[h] = df[:, h * (M // 2):(h + 1) * (M // 2)]

    def both(i, src_d, src_u, dst_d, dst_u, to, pair):
        return (remote(src_d, dst_d, rd_s.at[i], rd_r.at[i], to, pair),
                remote(src_u, dst_u, ru_s.at[i], ru_r.at[i], to, pair))

    tile = 384 if M % 384 == 0 else 128

    def grad_part(j, _):
        t = pl.ds(pl.multiple_of(j * tile, tile), tile)
        g = mm(vg[:, :HALF], wb[0, t, :], 1, 1) + mm(vg[:, HALF:], wb[1, t, :], 1, 1)
        xg_ref[:, t] = (g + ADAPT * mm(mid, dn_ref[t, :], 1, 1)).astype(BF16)
        return 0

    rounds = LOG + 2
    tiles = M // tile
    for i in range(rounds):
        if i <= LOG:
            at_half = 1 - p if i == 0 else p
            hdb[...] = hd[at_half].astype(BF16)
            hub[...] = hu[at_half].astype(BF16)
            if i == 0:
                to, pair = c, 1 - p
            else:
                bit = 1 << (i - 1)
                to, pair = jnp.where(lax.rem(c // bit, 2) == 0, c + bit, c - bit), p
            copies = both(i, hdb, hub, rd.at[i], ru.at[i], to, pair)
        else:
            copies = both(i, hd.at[p], hu.at[p], rfd, rfu, c, 1 - p)
        for copy in copies:
            copy.start()
        lax.fori_loop(tiles * i // rounds, tiles * (i + 1) // rounds, grad_part, 0)
        for copy in copies:
            copy.wait()
        if i <= LOG:
            mine_d = hd[p] if i == 0 else hdb[...].astype(F32)
            mine_u = hu[p] if i == 0 else hub[...].astype(F32)
            hd[p] = mine_d + rd[i].astype(F32)
            hu[p] = mine_u + ru[i].astype(F32)
    dd_ref[p] = hd[p]
    du_ref[p] = hu[p]
    dd_ref[1 - p] = rfd[...]
    du_ref[1 - p] = rfu[...]

    hop(0, c, w_ref.at[p, pl.ds(pl.multiple_of(y * U, 16), R - U), :], right).wait_send()
    hop(1, c, w_ref.at[p, pl.ds(pl.multiple_of(y * U, 16), R - U), :], left).wait_send()

    def ring_sent(s, _):
        slot = at(pos - s)

        @pl.when(s < NR)
        def _():
            hop(0, slot, block(slot), right).wait_send()
        to_partner(slot).wait_send()
        if U:
            to_group(slot).wait_send()
            rest_to_partner(slot).wait_send()

        @pl.when(s <= NL)
        def _():
            slot2 = at(pos + s)

            @pl.when(s < NL)
            def _():
                hop(1, slot2, block(slot2), left).wait_send()
            to_partner(slot2).wait_send()
            if U:
                to_group(slot2).wait_send()
                rest_to_partner(slot2).wait_send()
        return 0
    lax.fori_loop(1, NR + 1, ring_sent, 0)

    def sums_sent(i, _):
        sums(i).wait_send()
        return 0
    lax.fori_loop(1, 2 * n, sums_sent, 0)
    for d in range(1, D + 1):
        @pl.when(c + d < n)
        def _():
            label(d).wait_send()
    k_sent()
    for ch in range(NC):
        v_chains[ch][2]()
        parts_each(ch, lambda copy: copy.wait_send())
        for k in range(1, L + 1):
            @pl.when(c - 2 * k >= 0)
            def _():
                pz(ch, k).wait_send()


def shards(x, q, k, w, dn, up, g, plp, rlp, idx):
    n = lax.axis_size("ctx")
    T, width = k.shape[1], k.shape[2]
    rows = w.shape[0]
    R = -(-rows // 16) * 16
    model = x.shape[2]
    halo = WINDOW // T
    D = min(halo, n - 1)
    L = min(halo // 2, n // 2 - 1)
    NC = 8
    LOG = n.bit_length() - 1
    HALF = width // 2
    pad = R - rows
    M = n * R
    xs = x[0]
    if pad:
        xs = jnp.pad(xs.reshape(T, n, rows), ((0, 0), (0, 0), (0, pad))).reshape(T, M)
    ws = jnp.pad(w.reshape(rows, 2, HALF).transpose(1, 0, 2), ((0, 0), (0, pad), (0, 0)))
    dns = dn
    if pad:
        dns = jnp.pad(dn.reshape(n, rows, dn.shape[1]), ((0, 0), (0, pad), (0, 0))).reshape(M, dn.shape[1])
    lab = jnp.broadcast_to(idx.astype(F32), (SEGS, T))
    gap = jnp.broadcast_to(plp - rlp, (SEGS, T))
    rank = dn.shape[1]
    vm = pl.BlockSpec(memory_space=pltpu.VMEM)
    dma = pltpu.SemaphoreType.DMA
    xg, qg, kg, dd, du = pl.pallas_call(
        functools.partial(kernel, n, L, D, NC, LOG),
        out_shape=(
            jax.ShapeDtypeStruct((T, M), BF16),
            jax.ShapeDtypeStruct(q.shape[1:], BF16),
            jax.ShapeDtypeStruct(k.shape[1:], BF16),
            jax.ShapeDtypeStruct((2, rank, M // 2), F32),
            jax.ShapeDtypeStruct((2, rank, HALF), F32),
        ),
        in_specs=[vm] * 9,
        out_specs=[vm] * 5,
        scratch_shapes=[
            pltpu.VMEM((2, M, HALF), BF16),
            pltpu.VMEM((D + 1, T, width), BF16),
            pltpu.VMEM((D + 1, T, width), BF16),
            pltpu.VMEM((D + 1, SEGS, T), F32),
            pltpu.VMEM((2, n, SEGS, 128), F32),
            pltpu.VMEM(((D + 1) * T, 2 * T), F32),
            pltpu.VMEM((T, rank), BF16),
            pltpu.VMEM((D + 1, 2, T, width), BF16),
            pltpu.VMEM((2, T, width), F32),
            pltpu.VMEM((L + 1, 2, T, width), BF16),
            pltpu.VMEM((L + 1, 2, T, width), BF16),
            pltpu.VMEM((L + 1, 2, T, width), BF16),
            pltpu.VMEM((2, rank, M // 2), F32),
            pltpu.VMEM((2, rank, HALF), F32),
            pltpu.VMEM((rank, M // 2), BF16),
            pltpu.VMEM((rank, HALF), BF16),
            pltpu.VMEM((LOG + 1, rank, M // 2), BF16),
            pltpu.VMEM((LOG + 1, rank, HALF), BF16),
            pltpu.VMEM((rank, M // 2), F32),
            pltpu.VMEM((rank, HALF), F32),
            pltpu.VMEM((8, 2 * T), F32),
            dma((2, n)), dma((n,)), dma((n,)), dma((n,)), dma((n,)), dma((n,)), dma((n,)), dma((n,)),
            dma((1, L + 1)), dma((1, L + 1)), dma((1, D + 1)),
            dma((NC, L + 1)), dma((NC, L + 1)), dma((NC, D + 1)),
            dma((D + 1,)), dma((D + 1,)), dma((2 * n,)), dma((2, n)),
            dma((NC, L + 1)), dma((NC, L + 1)), dma((NC, L + 1)), dma((NC, L + 1)),
            dma((LOG + 2,)), dma((LOG + 2,)), dma((LOG + 2,)), dma((LOG + 2,)),
        ],
        compiler_params=pltpu.CompilerParams(
            collective_id=0, has_side_effects=True, vmem_limit_bytes=60 * 1024 * 1024),
    )(xs, q[0], k[0], ws, dns, up, g[0], lab, gap)
    input_grad = xg
    down = dd.transpose(0, 2, 1).reshape(M, rank)
    if pad:
        input_grad = xg.reshape(T, n, R)[:, :, :rows].reshape(T, model)
        down = down.reshape(n, R, rank)[:, :rows].reshape(model, rank)
    upg = du.transpose(1, 0, 2).reshape(rank, width)
    return input_grad[None], qg[None], kg[None], down, upg


def solution(mesh):
    tok = P(("grp", "pair"), "ctx", None)
    row = P(("grp", "pair"), "ctx")
    return jax.shard_map(
        shards,
        mesh=mesh,
        in_specs=(tok, tok, tok, P("ctx", None), P(), P(), tok, row, row, row),
        out_specs=(tok, tok, tok, P("grp", None), P("grp", None)),
        check_vma=False,
    )
```
